128 devices in a mesh: space: 16 (over y_hi, z, core), spec: 8 (over y_lo, x).
Axes of the slice: x: 4, y: 4 (y_hi: 2, y_lo: 2; y = y_hi * 2 + y_lo), z: 4, core: 2. Of those that a mesh axis runs over, the one named last changes fastest.
Arguments:
- spectrum: float32 [1296, 128, 128], P('spec', 'space'), may hold values from -6 to 6
- ocean_mask: int32 [128, 128], P('space'), may hold values 0 or 1
- depth_class: int32 [128, 128], P('space'), may hold values from 0 to 7
- freq_speed: float32 [36], replicated, may hold values from 0.15 to 0.45
- coupling: bfloat16 [1296, 1296], replicated, may hold values from -0.0390625 to 0.0390625
- source: bfloat16 [1296, 1296], replicated, may hold values from -0.0390625 to 0.0390625
- gain_table: float32 [8, 1296], replicated, may hold values from 0.5 to 2
Outputs:
- result: float32 [1296, 128, 128], P('spec', 'space')
The draws below stay inside these ranges and needn't reach their ends.
All inputs are finite; a program needn't handle non-finite values. No bound on the sum of `ocean_mask` on one device may be relied on, other than what follows from the above.
Results may differ from the reference program's by a relative error of at most 0.00088.
Values sent between devices are 32-bit elements; how exact they have to be, the bound alone decides.
A program may use at most 64 MiB of HBM per device.

```python
import math
import jax
import jax.numpy as jnp
from jax import lax

NDIR = 36
NFREQ = 36
BINS = 1296
NX = 128
NY = 128
CLASSES = 8
SUB = 2
ITERS = 4


def place_ends(result, stream_key, low, high):
    longest = result.shape.index(max(result.shape))
    spots = []
    for shift in (0, 1):
        where = [jax.random.randint(jax.random.fold_in(stream_key, axis), (), 0, length) for axis, length in enumerate(result.shape)]
        where[longest] = (where[longest] + shift) % result.shape[longest]
        spots.append(tuple(where))
    return result.at[spots[0]].set(low).at[spots[1]].set(high)


def block_scale(rng, extent, split, low, high):
    def one(axis_at, blocks):
        steps = jax.random.uniform(jax.random.fold_in(jax.random.fold_in(rng, 6), axis_at), (blocks,), jnp.float32, low / len(split), high / len(split))
        return jnp.repeat(jnp.exp(steps), extent[axis_at] // blocks).reshape((-1,) + (1,) * (len(extent) - axis_at - 1))

    factor_of = one(*split[0])
    for cut in split[1:]:
        factor_of = factor_of * one(*cut)
    return factor_of


def centred(rng, dims, scale, bound, cuts=(), held_as=jnp.bfloat16):
    result = scale * jax.random.normal(rng, dims, jnp.float32)
    if cuts:
        result = result * block_scale(rng, dims, cuts, -0.22, 0.18)
    return jnp.clip(result, -bound, bound).astype(held_as)


def setup_inputs(seed: int = 0) -> dict:
    streams_of = jax.random.split(jax.random.key(seed), 8)
    spectrum = centred(streams_of[0], (BINS, NY, NX), 1.0, 6.0, ((0, 8), (1, 16)), jnp.float32)
    ocean_mask = place_ends((jax.random.randint(streams_of[1], (NY, NX), 0, 5) < 4).astype(jnp.int32), jax.random.fold_in(streams_of[1], 1), 0, 1)
    depth_class = place_ends(jax.random.randint(streams_of[2], (NY, NX), 0, CLASSES), jax.random.fold_in(streams_of[2], 1), 0, CLASSES - 1).astype(jnp.int32)
    freq_speed = jnp.clip(jnp.exp(jax.random.uniform(streams_of[3], (NFREQ,), jnp.float32, math.log(0.15), math.log(0.45))), 0.15, 0.45)
    coupling = centred(streams_of[4], (BINS, BINS), (16 * BINS) ** -0.5, 0.0390625)
    source = centred(streams_of[5], (BINS, BINS), (16 * BINS) ** -0.5, 0.0390625)
    gain_table = jnp.clip(jax.random.uniform(streams_of[6], (CLASSES, BINS), jnp.float32, 0.5, 2.0), 0.5, 2.0)
    return {"spectrum": spectrum, "ocean_mask": ocean_mask, "depth_class": depth_class, "freq_speed": freq_speed, "coupling": coupling, "source": source, "gain_table": gain_table}


def velocities(freq_speed):
    bin_index = jnp.arange(NDIR * NFREQ)
    frequency = bin_index // NDIR
    heading = 2.0 * jnp.pi * ((bin_index % NDIR).astype(jnp.float32) + 0.5) / NDIR
    group_speed = freq_speed[frequency]
    return group_speed * jnp.cos(heading), group_speed * jnp.sin(heading)


def upwind(padded, speed_x, speed_y, sea_cells):
    interior = padded[:, 1:-1]
    plus_x = jnp.maximum(speed_x, 0.0)[:, None, None]
    minus_x = jnp.minimum(speed_x, 0.0)[:, None, None]
    plus_y = jnp.maximum(speed_y, 0.0)[:, None, None]
    minus_y = jnp.minimum(speed_y, 0.0)[:, None, None]
    padded_x = jnp.pad(interior, ((0, 0), (0, 0), (1, 1)))
    flux_x = plus_x * padded_x[:, :, :-1] + minus_x * padded_x[:, :, 1:]
    flux_y = plus_y * padded[:, :-1] + minus_y * padded[:, 1:]
    updated = interior - (flux_x[:, :, 1:] - flux_x[:, :, :-1]) - (flux_y[:, 1:] - flux_y[:, :-1])
    return updated * sea_cells


def advect(spectra, speed_x, speed_y, sea_cells):
    for substep in range(SUB):
        padded = jnp.pad(spectra, ((0, 0), (1, 1), (0, 0)))
        spectra = upwind(padded, speed_x, speed_y, sea_cells)
    return spectra


def tendency(spectra, coupling, source, cell_gains):
    rounded = spectra.astype(jnp.bfloat16).astype(jnp.float32)
    turned = jnp.dot(coupling.astype(jnp.float32).T, rounded, precision=lax.Precision.HIGHEST)
    forced = jnp.dot(source.astype(jnp.float32).T, rounded, precision=lax.Precision.HIGHEST)
    return cell_gains * turned + forced


def heun_step(spectra, coupling, source, cell_gains):
    slope_one = tendency(spectra, coupling, source, cell_gains)
    slope_two = tendency(spectra + slope_one, coupling, source, cell_gains)
    return spectra + 0.5 * (slope_one + slope_two)


def reference(spectrum, ocean_mask, depth_class, freq_speed, coupling, source, gain_table):
    speed_x, speed_y = velocities(freq_speed)
    sea_cells = ocean_mask.astype(jnp.float32)
    cell_gains = jnp.take(gain_table, depth_class.reshape(-1), axis=0).T
    spectra = spectrum
    for outer in range(ITERS):
        spectra = advect(spectra, speed_x, speed_y, sea_cells)
        flat_cells = heun_step(spectra.reshape(spectra.shape[0], -1), coupling, source, cell_gains)
        spectra = flat_cells.reshape(spectra.shape)
        spectra = advect(spectra, speed_x, speed_y, sea_cells)
    return spectra
```

```python
import functools
import math

import jax
import jax.numpy as jnp
from jax import lax
from jax.experimental import pallas as pl
from jax.experimental.pallas import tpu as pltpu
from jax.sharding import PartitionSpec as P

MESH = pl.DeviceIdType.MESH
F32, BF16, I32 = jnp.float32, jnp.bfloat16, jnp.int32
BINS, NDIR, NFREQ, CLASSES = 1296, 36, 36, 8
ITERS = 4
NSPEC, LOCAL = 8, 162
SLOT = 48
FULL = (5, 5, 4, 4)
BASE = (0, 48, 96, 136)
KEPT = (48, 48, 40, 40)
ROWS = 176
LOWX, LOWY = (True, False, False, True), (True, True, False, False)
PAIRS = ((0, 0), (1, 0), (1, 1), (2, 1), (3, 1), (3, 2), (4, 2), (5, 2))
PHASES = ITERS + 1


def off_j(q):
    return 4 if LOWY[q] else 0


def off_i(q):
    return 8 if LOWX[q] else 0


def block_of(r, half):
    low = lax.rem(r // 4 + half, 2)
    x = lax.rem(r, 4)
    return jnp.where(low == 0, x, 7 - x)


def owner_of(c, half):
    x = jnp.where(c < 4, c, 7 - c)
    return lax.rem(c // 4 + half, 2) * 4 + x


def swap_blocks(parts):
    lane = lax.broadcasted_iota(I32, parts[0].shape, 1)
    for h in (4, 2, 1):
        keep = (lane & (16 * h)) == 0
        new = list(parts)
        for j in range(8):
            if j & h == 0:
                a, b = parts[j], parts[j + h]
                new[j] = jnp.where(keep, a, pltpu.roll(b, 16 * h, 1))
                new[j + h] = jnp.where(keep, pltpu.roll(a, 128 - 16 * h, 1), b)
        parts = new
    return parts


def local_bin(rel, idx):
    many = rel < 2
    whole = jnp.where(many, 40, 32)
    runs = jnp.where(many, 5, 4)
    first = 36 * (idx >> 3) + (idx & 7)
    last = 36 * (idx - whole) + 8
    return jnp.where(idx < whole, first + 9 * rel, jnp.where(idx < whole + runs, last + 9 * rel, -10000))


def places(q, g, shape):
    slot = 128 * g + lax.broadcasted_iota(I32, shape, len(shape) - 1)
    r = jnp.zeros_like(slot)
    for k in range(1, 8):
        r = r + (slot >= SLOT * k).astype(I32)
    return r, q ^ (2 * (r & 1)), slot - SLOT * r


def kernel(ns, x_ref, mask_ref, class_ref, speed_ref, coupling_ref, source_ref, gain_ref, out_ref,
           natural, turned, weights, pick, e0, e1, slope, xb, yb, gains, gain_rows, mask, coef,
           send_a, land_a, land_b, xs, cs, yl, xl, cl, tile, strip, mask_own, mask_land,
           w_sem, a_send, a_recv, b_send, b_recv, h_send, h_recv, m_send, m_recv):
    r = lax.axis_index("spec")
    s = lax.axis_index("space")
    half = s // (ns // 2)
    c = block_of(r, half)

    def at(dc, ds):
        cc, ss = jnp.clip(c + dc, 0, NSPEC - 1), jnp.clip(s + ds, 0, ns - 1)
        return (ss, owner_of(cc, ss // (ns // 2)))

    def there(dc, ds):
        ok = None
        for cond in ([c + dc >= 0, c + dc < NSPEC] if dc else []) + ([s + ds >= 0, s + ds < ns] if ds else []):
            ok = cond if ok is None else jnp.logical_and(ok, cond)
        return ok

    loads = [pltpu.make_async_copy(ref, natural.at[m], w_sem.at[m]) for m, ref in enumerate((coupling_ref, source_ref))]
    for copy in loads:
        copy.start()
    barrier = pltpu.get_barrier_semaphore()
    around = [(dc, ds) for ds in (-1, 1) for dc in (-1, 0, 1)]
    for k in range(1, NSPEC):
        pl.semaphore_signal(barrier, inc=1, device_id=(s, lax.rem(r + k, NSPEC)), device_id_type=MESH)
    for dc, ds in around:
        @pl.when(there(dc, ds))
        def _():
            pl.semaphore_signal(barrier, inc=1, device_id=at(dc, ds), device_id_type=MESH)

    mask_own[...] = mask_ref[...].astype(F32)

    for rel in range(4):
        def pack(f, _, rel=rel):
            parts = [x_ref[pl.ds((36 * f + 9 * rel) * 8 + j, 8, stride=8), :] for j in range(8)]
            for cc, part in enumerate(swap_blocks(parts)):
                send_a[cc, pl.ds(pl.multiple_of(BASE[rel] + 8 * f, 8), 8), :] = part
            return 0
        lax.fori_loop(0, FULL[rel], pack, 0)
        n = FULL[rel]
        parts = [x_ref[pl.ds((9 * rel + 8) * 8 + j, n, stride=288), :] for j in range(8)]
        for cc, part in enumerate(swap_blocks(parts)):
            send_a[cc, BASE[rel] + 8 * n:BASE[rel] + 8 * n + 8, :] = jnp.zeros((8, 128), F32)
            send_a[cc, BASE[rel] + 8 * n:BASE[rel] + 9 * n, :] = part

    beside = (c > 0).astype(I32) + (c < NSPEC - 1).astype(I32)
    beyond = (s > 0).astype(I32) + (s < ns - 1).astype(I32)
    pl.semaphore_wait(barrier, NSPEC - 1 + beyond * (1 + beside))

    def a_copy(k, incoming=False):
        peer = lax.rem(r + k, NSPEC)
        return pltpu.make_async_remote_copy(
            src_ref=send_a.at[block_of(peer, half)], dst_ref=land_a.at[peer if incoming else r],
            send_sem=a_send.at[k], recv_sem=a_recv.at[peer if incoming else r],
            device_id=(s, peer), device_id_type=MESH)

    for k in range(1, NSPEC):
        a_copy(k).start()
    own_a = pltpu.make_async_copy(send_a.at[c], land_a.at[r], a_send.at[0])
    own_a.start()

    def mask_copy(ds, incoming=False):
        k = (1 if ds < 0 else 0) if not incoming else (0 if ds < 0 else 1)
        return pltpu.make_async_remote_copy(
            src_ref=mask_own, dst_ref=mask_land.at[k], send_sem=m_send.at[k], recv_sem=m_recv.at[k],
            device_id=at(0, ds), device_id_type=MESH)

    for ds in (-1, 1):
        @pl.when(there(0, ds))
        def _():
            mask_copy(ds).start()

    def clear(qg, _):
        e0[qg] = jnp.zeros((12, 24, 128), F32)
        e1[qg] = jnp.zeros((12, 24, 128), F32)
        return 0
    lax.fori_loop(0, 12, clear, 0)

    row = lax.broadcasted_iota(I32, (16, 128), 0)
    quad = (row >= 3).astype(I32) + (row >= 6).astype(I32) + (row >= 9).astype(I32)
    home, rel, idx = places(quad, row - 3 * quad, (16, 128))
    here = local_bin(rel, idx)
    many = rel < 2
    whole = jnp.where(many, 40, 32)
    run = jnp.where(idx < whole, idx >> 3, idx - whole)
    step = jnp.where(idx < whole, idx & 7, 8)
    freq = ((9 * home) >> 1) + run + jnp.where(many, 0, home & 1)
    group_speed = jnp.zeros((16, 128), F32)
    for k in range(NFREQ):
        group_speed = jnp.where(freq == k, speed_ref[k], group_speed)
    group_speed = jnp.where(here >= 0, group_speed, 0.0)
    cosine, sine = jnp.zeros((16, 128), F32), jnp.zeros((16, 128), F32)
    for k in range(9):
        cosine = jnp.where(step == k, math.cos(2.0 * math.pi * (k + 0.5) / NDIR), cosine)
        sine = jnp.where(step == k, math.sin(2.0 * math.pi * (k + 0.5) / NDIR), sine)
    even = (quad & 1) == 0
    ax = group_speed * jnp.where(even, cosine, sine)
    ay = group_speed * jnp.where(even, sine, cosine)
    coef[0] = 1.0 - ax - ay
    coef[1] = ax
    coef[2] = ay

    for k, (t, g) in enumerate(PAIRS):
        rows = 16 if t == 5 else 256
        for q in range(4):
            home, rel, idx = places(jnp.full((1, 128), q, I32), g, (1, 128))
            want = LOCAL * home + local_bin(rel, idx) - 256 * t
            hit = lax.broadcasted_iota(I32, (rows, 128), 0) == want
            pick[k, 0:rows, 128 * q:128 * q + 128] = jnp.where(hit, 1.0, 0.0).astype(BF16)

    def to_quadrants(lhs, g):
        total = None
        for k, (t, gg) in enumerate(PAIRS):
            if gg == g:
                rows = 16 if t == 5 else 256
                term = jnp.dot(lhs(256 * t, rows), pick[k, 0:rows, :], preferred_element_type=F32)
                total = term if total is None else total + term
        return total

    table = gain_ref[...]
    high = table.astype(BF16).astype(F32)
    mid = (table - high).astype(BF16).astype(F32)
    low = table - high - mid
    thirds = jnp.concatenate([high, mid, low, jnp.zeros_like(low)], axis=0).astype(BF16)
    for g in range(3):
        total = to_quadrants(lambda at_, n: thirds[:, at_:at_ + n], g)
        for q in range(4):
            part = total[:, 128 * q:128 * q + 128]
            gain_rows[3 * q + g] = part[0:8] + part[8:16] + part[16:24]

    for copy in loads:
        copy.wait()
    for m in range(2):
        def columns(k, _, m=m):
            rows = pl.ds(pl.multiple_of(144 * k, 16), 144)
            for g in range(3):
                total = to_quadrants(lambda at_, n: natural[m, rows, at_:at_ + n], g).astype(BF16)
                for q in range(4):
                    turned[3 * q + g, rows, 128 * m:128 * m + 128] = total[:, 128 * q:128 * q + 128]
            return 0
        lax.fori_loop(0, 9, columns, 0)

    for rr in range(NSPEC):
        blocks = []
        for q in range(4):
            place = lax.broadcasted_iota(I32, (SLOT, 176), 0)
            want = local_bin(jnp.full((SLOT, 176), q ^ (2 * (rr & 1)), I32), place) + 2 * rr
            hit = lax.broadcasted_iota(I32, (SLOT, 176), 1) == want
            blocks.append(jnp.where(hit, 1.0, 0.0).astype(BF16))
        onehot = jnp.concatenate(blocks, axis=0)

        def lines(qg, _, rr=rr, onehot=onehot):
            got = jnp.dot(onehot, turned[qg, 160 * rr:160 * rr + 176, :], preferred_element_type=F32).astype(BF16)
            for q in range(4):
                weights[qg, 384 * q + SLOT * rr:384 * q + SLOT * rr + SLOT, :] = got[SLOT * q:SLOT * q + SLOT]
            return 0
        lax.fori_loop(0, 12, lines, 0, unroll=2)

    for k, ds in ((0, -1), (1, 1)):
        @pl.when(there(0, ds))
        def _():
            mask_copy(ds, incoming=True).wait_recv()
            mask_copy(ds).wait_send()
            tile[16 * k:16 * k + 8, :] = mask_land[k]

        @pl.when(jnp.logical_not(there(0, ds)))
        def _():
            tile[16 * k:16 * k + 8, :] = jnp.zeros((8, 128), F32)
    tile[8:16, :] = mask_own[...]
    tile[24:32, :] = class_ref[...].astype(F32)
    tile[32:128, :] = jnp.zeros((96, 128), F32)
    strip[0:8, :] = jnp.zeros((8, 128), F32)
    strip[136:152, :] = jnp.zeros((16, 128), F32)
    strip[8:136, :] = tile[...].T
    near = strip[pl.ds(pl.multiple_of(16 * c, 16), 32), :]
    for j in range(16):
        mask[j] = jnp.broadcast_to(near[:, j + 4:j + 5], (32, 128))
    for j in range(8):
        kind = jnp.broadcast_to(near[8:24, 24 + j:25 + j], (16, 128))

        def fill(qg, _, j=j, kind=kind):
            value = jnp.zeros((16, 128), F32)
            for k in range(CLASSES):
                value = jnp.where(kind == float(k), gain_rows[qg, k:k + 1, :], value)
            gains[qg, 16 * j:16 * j + 16, :] = value
            return 0
        lax.fori_loop(0, 12, fill, 0)

    own_a.wait()
    for k in range(1, NSPEC):
        a_copy(k, incoming=True).wait_recv()
    for q in range(4):
        for g in range(3):
            pieces = []
            for rr in range(NSPEC):
                a, b = max(SLOT * rr, 128 * g) - SLOT * rr, min(SLOT * rr + SLOT, 128 * g + 128) - SLOT * rr
                if a >= b:
                    continue
                rel = q ^ (2 * (rr & 1))
                cut = min(b, KEPT[rel])
                if a < cut:
                    pieces.append(land_a[rr, BASE[rel] + a:BASE[rel] + cut, :])
                if cut < b:
                    pieces.append(jnp.zeros((b - max(a, cut), 128), F32))
            e0[3 * q + g, off_j(q):off_j(q) + 8, off_i(q):off_i(q) + 16, :] = (
                jnp.concatenate(pieces, axis=0).T.reshape(8, 16, 128))

    def heading(q):
        return (1 if LOWX[q] else -1), (1 if LOWY[q] else -1)

    def edge(q, kind):
        dx, dy = heading(q)
        return ((0, dy), (dx, 0), (dx, dy))[kind]

    def edge_copy(p, q, kind):
        dc, ds = edge(q, kind)
        groups = pl.ds(3 * q, 3)
        if kind == 0:
            src = e0.at[groups, pl.ds(8 if LOWY[q] else 0, 4), pl.ds(off_i(q), 16)]
            dst = yl.at[p, groups]
        elif kind == 1:
            src, dst = xs.at[groups], xl.at[p, groups]
        else:
            src, dst = cs.at[groups], cl.at[p, groups]
        return pltpu.make_async_remote_copy(
            src_ref=src, dst_ref=dst, send_sem=h_send.at[p, q, kind], recv_sem=h_recv.at[p, q, kind],
            device_id=at(dc, ds), device_id_type=MESH)

    def send_edges(p, q):
        i = 20 if LOWX[q] else 0
        jc = 8 if LOWY[q] else 0

        def pack(g, _):
            qg = 3 * q + g
            for j in range(8):
                xs[qg, j // 2, 4 * (j % 2):4 * (j % 2) + 4, :] = e0[qg, off_j(q) + j, i:i + 4, :]
            for j in range(4):
                cs[qg, j // 2, 4 * (j % 2):4 * (j % 2) + 4, :] = e0[qg, jc + j, i:i + 4, :]
            return 0
        lax.fori_loop(0, 3, pack, 0, unroll=3)
        for kind in range(3):
            @pl.when(there(*edge(q, kind)))
            def _():
                edge_copy(p, q, kind).start()

    def take_edges(p, q):
        i = 4 if LOWX[q] else 16
        jh = 0 if LOWY[q] else 8
        for kind in range(3):
            dc, ds = edge(q, kind)

            @pl.when(there(dc, ds))
            def _():
                edge_copy(p, q, kind).wait_send()

            @pl.when(there(-dc, -ds))
            def _():
                edge_copy(p, q, kind).wait_recv()

                def unpack(g, _):
                    qg = 3 * q + g
                    if kind == 0:
                        e0[qg, jh:jh + 4, off_i(q):off_i(q) + 16, :] = yl[p, qg]
                    else:
                        for j in range(8 if kind == 1 else 4):
                            got = (xl if kind == 1 else cl)[p, qg, j // 2, 4 * (j % 2):4 * (j % 2) + 4, :]
                            e0[qg, (off_j(q) if kind == 1 else jh) + j, i:i + 4, :] = got
                    return 0
                lax.fori_loop(0, 3, unpack, 0, unroll=3)

    def substep(q, t):
        src, dst = (e0, e1) if t % 2 == 0 else (e1, e0)
        if LOWY[q]:
            j0, n, dj, jm = t + 1, 11 - t, -1, 0
        else:
            j0, n, dj, jm = 0, 11 - t, 1, 4
        if LOWX[q]:
            di, im, starts = -1, 0, (8, 16) + (() if t == 3 else (1,))
        else:
            di, im, starts = 1, 8, (0, 8) + (() if t == 3 else (15,))

        def body(g, _):
            qg = 3 * q + g
            c0 = coef[0, pl.ds(qg, 1), :].reshape(1, 1, 128)
            cx = coef[1, pl.ds(qg, 1), :].reshape(1, 1, 128)
            cy = coef[2, pl.ds(qg, 1), :].reshape(1, 1, 128)
            for i in starts:
                mid = src[qg, j0:j0 + n, i:i + 8, :]
                along = src[qg, j0:j0 + n, i + di:i + di + 8, :]
                across = src[qg, j0 + dj:j0 + dj + n, i:i + 8, :]
                sea = mask[j0 + jm:j0 + jm + n, i + im:i + im + 8, :]
                dst[qg, j0:j0 + n, i:i + 8, :] = (c0 * mid + cx * along + cy * across) * sea
            return 0
        lax.fori_loop(0, 3, body, 0)

    def interior(q):
        return slice(off_j(q), off_j(q) + 8), slice(off_i(q), off_i(q) + 16)

    def place(qg):
        q = (qg >= 3).astype(I32) + (qg >= 6).astype(I32) + (qg >= 9).astype(I32)
        j = jnp.where(q < 2, 4, 0)
        i = pl.multiple_of(jnp.where(jnp.logical_or(q == 0, q == 3), 8, 0), 8)
        return pl.ds(j, 8), pl.ds(i, 16)

    def couple():
        for q in range(4):
            js, is_ = interior(q)
            for g in range(3):
                qg = 3 * q + g
                xb[:, 128 * qg:128 * qg + 128] = e0[qg, js, is_, :].reshape(128, 128).astype(BF16)

        def first(qg, _):
            got = jnp.dot(xb[...], weights[qg], preferred_element_type=F32)
            change = gains[qg] * got[:, :128] + got[:, 128:]
            slope[qg] = change
            js, is_ = place(qg)
            state = e0[qg, js, is_, :].reshape(128, 128)
            yb[:, pl.ds(pl.multiple_of(128 * qg, 128), 128)] = (state + change).astype(BF16)
            return 0
        lax.fori_loop(0, 12, first, 0, unroll=4)

        def second(qg, _):
            got = jnp.dot(yb[...], weights[qg], preferred_element_type=F32)
            change = gains[qg] * got[:, :128] + got[:, 128:]
            js, is_ = place(qg)
            state = e0[qg, js, is_, :].reshape(128, 128)
            e0[qg, js, is_, :] = (state + 0.5 * (slope[qg] + change)).reshape(8, 16, 128)
            return 0
        lax.fori_loop(0, 12, second, 0, unroll=4)

    def phase(p, _):
        for q in range(4):
            send_edges(p, q)
        for q in range(4):
            take_edges(p, q)

        @pl.when(jnp.logical_and(p > 0, p < PHASES - 1))
        def _():
            for q in range(4):
                substep(q, 0)
                substep(q, 1)
        for q in range(4):
            substep(q, 2)
            substep(q, 3)

        @pl.when(p < PHASES - 1)
        def _():
            couple()
        return 0

    lax.fori_loop(0, PHASES, phase, 0)

    for k in range(1, NSPEC):
        a_copy(k).wait_send()
    for q in range(4):
        js, is_ = interior(q)
        for g in range(3):
            block = e0[3 * q + g, js, is_, :].reshape(128, 128).T
            for rr in range(NSPEC):
                a, b = max(SLOT * rr, 128 * g), min(SLOT * rr + SLOT, 128 * g + 128)
                rel = q ^ (2 * (rr & 1))
                b = min(b, SLOT * rr + KEPT[rel])
                if a < b:
                    send_a[rr, BASE[rel] + a - SLOT * rr:BASE[rel] + b - SLOT * rr, :] = block[a - 128 * g:b - 128 * g]

    def b_copy(k, incoming=False):
        peer = lax.rem(r + k, NSPEC)
        slot = block_of(peer, half) if incoming else c
        return pltpu.make_async_remote_copy(
            src_ref=send_a.at[peer], dst_ref=land_b.at[slot], send_sem=b_send.at[k], recv_sem=b_recv.at[slot],
            device_id=(s, peer), device_id_type=MESH)

    for k in range(1, NSPEC):
        b_copy(k).start()
    own_b = pltpu.make_async_copy(send_a.at[r], land_b.at[c], b_send.at[0])
    own_b.start()
    own_b.wait()
    for k in range(1, NSPEC):
        b_copy(k, incoming=True).wait_recv()
    for rel in range(4):
        def unpack(f, _, rel=rel):
            rows = pl.ds(pl.multiple_of(BASE[rel] + 8 * f, 8), 8)
            parts = swap_blocks([land_b[cc, rows, :] for cc in range(8)])
            for j in range(8):
                out_ref[pl.ds((36 * f + 9 * rel) * 8 + j, 8, stride=8), :] = parts[j]
            return 0
        lax.fori_loop(0, FULL[rel], unpack, 0)
        n = FULL[rel]
        parts = swap_blocks([land_b[cc, BASE[rel] + 8 * n:BASE[rel] + 9 * n, :] for cc in range(8)])
        for j in range(8):
            out_ref[pl.ds((9 * rel + 8) * 8 + j, n, stride=288), :] = parts[j]
    for k in range(1, NSPEC):
        b_copy(k).wait_send()


def shards(ns, spectrum, ocean_mask, depth_class, freq_speed, coupling, source, gain_table):
    vmem, hbm = pl.BlockSpec(memory_space=pltpu.VMEM), pl.BlockSpec(memory_space=pl.ANY)
    dma = pltpu.SemaphoreType.DMA
    out = pl.pallas_call(
        functools.partial(kernel, ns),
        out_shape=jax.ShapeDtypeStruct((LOCAL * 8, 128), F32),
        in_specs=[vmem, vmem, vmem, pl.BlockSpec(memory_space=pltpu.SMEM), hbm, hbm, vmem],
        out_specs=vmem,
        scratch_shapes=[
            pltpu.VMEM((2, BINS, BINS), BF16),
            pltpu.VMEM((12, BINS, 256), BF16),
            pltpu.VMEM((12, 1536, 256), BF16),
            pltpu.VMEM((8, 256, 512), BF16),
            pltpu.VMEM((12, 12, 24, 128), F32),
            pltpu.VMEM((12, 12, 24, 128), F32),
            pltpu.VMEM((12, 128, 128), F32),
            pltpu.VMEM((128, 1536), BF16),
            pltpu.VMEM((128, 1536), BF16),
            pltpu.VMEM((12, 128, 128), F32),
            pltpu.VMEM((12, 8, 128), F32),
            pltpu.VMEM((16, 32, 128), F32),
            pltpu.VMEM((3, 16, 128), F32),
            pltpu.VMEM((8, ROWS, 128), F32),
            pltpu.VMEM((8, ROWS, 128), F32),
            pltpu.VMEM((8, ROWS, 128), F32),
            pltpu.VMEM((12, 4, 8, 128), F32),
            pltpu.VMEM((12, 2, 8, 128), F32),
            pltpu.VMEM((PHASES, 12, 4, 16, 128), F32),
            pltpu.VMEM((PHASES, 12, 4, 8, 128), F32),
            pltpu.VMEM((PHASES, 12, 2, 8, 128), F32),
            pltpu.VMEM((128, 128), F32),
            pltpu.VMEM((152, 128), F32),
            pltpu.VMEM((8, 128), F32),
            pltpu.VMEM((2, 8, 128), F32),
            dma((2,)), dma((8,)), dma((8,)), dma((8,)), dma((8,)),
            dma((PHASES, 4, 3)), dma((PHASES, 4, 3)), dma((2,)), dma((2,)),
        ],
        compiler_params=pltpu.CompilerParams(
            collective_id=0, has_side_effects=True, vmem_limit_bytes=56 * 2**20),
        cost_estimate=pl.CostEstimate(flops=12 * 10**9, bytes_accessed=9 * 10**6, transcendentals=0),
        name="wave_steps",
    )(spectrum.reshape(LOCAL * 8, 128), ocean_mask, depth_class, freq_speed, coupling, source, gain_table)
    return out.reshape(LOCAL, 8, 128)


def solution(mesh):
    placed = (P("spec", "space", None), P("space", None), P("space", None), P(), P(), P(), P())
    return jax.shard_map(
        functools.partial(shards, mesh.shape["space"]), mesh=mesh, in_specs=placed,
        out_specs=P("spec", "space", None), check_vma=False)
```

```python
import functools
import math

import jax
import jax.numpy as jnp
from jax import lax
from jax.experimental import pallas as pl
from jax.experimental.pallas import tpu as pltpu
from jax.sharding import PartitionSpec as P

MESH = pl.DeviceIdType.MESH
F32, BF16, I32 = jnp.float32, jnp.bfloat16, jnp.int32
BINS, NDIR, NFREQ, CLASSES = 1296, 36, 36, 8
ITERS = 4
NSPEC, LOCAL = 8, 162
SLOT = 48
FULL = (5, 5, 4, 4)
BASE = (0, 48, 96, 136)
KEPT = (48, 48, 40, 40)
ROWS = 176
QUADS = (0, 2, 1, 3)
LOWX, LOWY = (True, False, False, True), (True, False, True, False)
PAIRS = ((0, 0), (1, 0), (1, 1), (2, 1), (3, 1), (3, 2), (4, 2), (5, 2))
PHASES = ITERS + 1


def off_j(q):
    return 4 if LOWY[q] else 0


def off_i(q):
    return 8 if LOWX[q] else 0


def block_of(r, half):
    low = lax.rem(r // 4 + half, 2)
    x = lax.rem(r, 4)
    return jnp.where(low == 0, x, 7 - x)


def owner_of(c, half):
    x = jnp.where(c < 4, c, 7 - c)
    return lax.rem(c // 4 + half, 2) * 4 + x


def swap_blocks(parts):
    lane = lax.broadcasted_iota(I32, parts[0].shape, 1)
    for h in (4, 2, 1):
        keep = (lane & (16 * h)) == 0
        new = list(parts)
        for j in range(8):
            if j & h == 0:
                a, b = parts[j], parts[j + h]
                new[j] = jnp.where(keep, a, pltpu.roll(b, 16 * h, 1))
                new[j + h] = jnp.where(keep, pltpu.roll(a, 128 - 16 * h, 1), b)
        parts = new
    return parts


def local_bin(rel, idx):
    many = rel < 2
    whole = jnp.where(many, 40, 32)
    runs = jnp.where(many, 5, 4)
    first = 36 * (idx >> 3) + (idx & 7)
    last = 36 * (idx - whole) + 8
    return jnp.where(idx < whole, first + 9 * rel, jnp.where(idx < whole + runs, last + 9 * rel, -10000))


def places(q, g, shape):
    slot = 128 * g + lax.broadcasted_iota(I32, shape, len(shape) - 1)
    r = jnp.zeros_like(slot)
    for k in range(1, 8):
        r = r + (slot >= SLOT * k).astype(I32)
    return r, q ^ (2 * (r & 1)), slot - SLOT * r


def relative(q, r):
    return QUADS[q] ^ (2 * (r & 1))


def kernel(ns, x_ref, mask_ref, class_ref, speed_ref, coupling_ref, source_ref, gain_ref, out_ref,
           natural, turned, weights, pick, e0, e1, slope, part, xb, yb, gains, gain_rows, mask, coef,
           send_a, land_a, land_b, xs, cs, yl, xl, cl, tile, strip, kind, mask_own, mask_land,
           w_sem, a_send, a_recv, b_send, b_recv, h_send, h_recv, m_send, m_recv):
    r = lax.axis_index("spec")
    s = lax.axis_index("space")
    half = s // (ns // 2)
    c = block_of(r, half)

    def at(dc, ds):
        cc, ss = jnp.clip(c + dc, 0, NSPEC - 1), jnp.clip(s + ds, 0, ns - 1)
        return (ss, owner_of(cc, ss // (ns // 2)))

    def there(dc, ds):
        ok = None
        for cond in ([c + dc >= 0, c + dc < NSPEC] if dc else []) + ([s + ds >= 0, s + ds < ns] if ds else []):
            ok = cond if ok is None else jnp.logical_and(ok, cond)
        return ok

    loads = [pltpu.make_async_copy(ref, natural.at[m], w_sem.at[m]) for m, ref in enumerate((coupling_ref, source_ref))]
    for copy in loads:
        copy.start()
    barrier = pltpu.get_barrier_semaphore()
    around = [(dc, ds) for ds in (-1, 1) for dc in (-1, 0, 1)]
    for k in range(1, NSPEC):
        pl.semaphore_signal(barrier, inc=1, device_id=(s, lax.rem(r + k, NSPEC)), device_id_type=MESH)
    for dc, ds in around:
        @pl.when(there(dc, ds))
        def _():
            pl.semaphore_signal(barrier, inc=1, device_id=at(dc, ds), device_id_type=MESH)

    mask_own[...] = mask_ref[...].astype(F32)

    for rel in range(4):
        for f in range(FULL[rel]):
            parts = [x_ref[pl.ds((36 * f + 9 * rel) * 8 + j, 8, stride=8), :] for j in range(8)]
            for cc, block in enumerate(swap_blocks(parts)):
                send_a[cc, BASE[rel] + 8 * f:BASE[rel] + 8 * f + 8, :] = block
        n = FULL[rel]
        parts = [x_ref[pl.ds((9 * rel + 8) * 8 + j, n, stride=288), :] for j in range(8)]
        for cc, block in enumerate(swap_blocks(parts)):
            send_a[cc, BASE[rel] + 8 * n:BASE[rel] + 8 * n + 8, :] = jnp.zeros((8, 128), F32)
            send_a[cc, BASE[rel] + 8 * n:BASE[rel] + 9 * n, :] = block

    beside = (c > 0).astype(I32) + (c < NSPEC - 1).astype(I32)
    beyond = (s > 0).astype(I32) + (s < ns - 1).astype(I32)
    pl.semaphore_wait(barrier, NSPEC - 1 + beyond * (1 + beside))

    def a_copy(k, incoming=False):
        peer = lax.rem(r + k, NSPEC)
        return pltpu.make_async_remote_copy(
            src_ref=send_a.at[block_of(peer, half)], dst_ref=land_a.at[peer if incoming else r],
            send_sem=a_send.at[k], recv_sem=a_recv.at[peer if incoming else r],
            device_id=(s, peer), device_id_type=MESH)

    for k in range(1, NSPEC):
        a_copy(k).start()
    own_a = pltpu.make_async_copy(send_a.at[c], land_a.at[r], a_send.at[0])
    own_a.start()

    def mask_copy(ds, incoming=False):
        k = (1 if ds < 0 else 0) if not incoming else (0 if ds < 0 else 1)
        return pltpu.make_async_remote_copy(
            src_ref=mask_own, dst_ref=mask_land.at[k], send_sem=m_send.at[k], recv_sem=m_recv.at[k],
            device_id=at(0, ds), device_id_type=MESH)

    for ds in (-1, 1):
        @pl.when(there(0, ds))
        def _():
            mask_copy(ds).start()

    def clear(qg, _):
        e0[qg] = jnp.zeros((12, 24, 128), F32)
        e1[qg] = jnp.zeros((12, 24, 128), F32)
        return 0
    lax.fori_loop(0, 12, clear, 0)

    row = lax.broadcasted_iota(I32, (16, 128), 0)
    quad = (row >= 3).astype(I32) + (row >= 6).astype(I32) + (row >= 9).astype(I32)
    group = row - 3 * quad
    quad = jnp.where(quad == 1, 2, jnp.where(quad == 2, 1, quad))
    home, rel, idx = places(quad, group, (16, 128))
    here = local_bin(rel, idx)
    many = rel < 2
    whole = jnp.where(many, 40, 32)
    run = jnp.where(idx < whole, idx >> 3, idx - whole)
    step = jnp.where(idx < whole, idx & 7, 8)
    freq = ((9 * home) >> 1) + run + jnp.where(many, 0, home & 1)
    group_speed = jnp.zeros((16, 128), F32)
    for k in range(NFREQ):
        group_speed = jnp.where(freq == k, speed_ref[k], group_speed)
    group_speed = jnp.where(here >= 0, group_speed, 0.0)
    cosine, sine = jnp.zeros((16, 128), F32), jnp.zeros((16, 128), F32)
    for k in range(9):
        cosine = jnp.where(step == k, math.cos(2.0 * math.pi * (k + 0.5) / NDIR), cosine)
        sine = jnp.where(step == k, math.sin(2.0 * math.pi * (k + 0.5) / NDIR), sine)
    even = (quad & 1) == 0
    ax = group_speed * jnp.where(even, cosine, sine)
    ay = group_speed * jnp.where(even, sine, cosine)
    coef[0] = 1.0 - ax - ay
    coef[1] = ax
    coef[2] = ay

    for k, (t, g) in enumerate(PAIRS):
        rows = 16 if t == 5 else 256
        for q in range(4):
            home, rel, idx = places(jnp.full((1, 128), QUADS[q], I32), g, (1, 128))
            want = LOCAL * home + local_bin(rel, idx) - 256 * t
            hit = lax.broadcasted_iota(I32, (rows, 128), 0) == want
            pick[k, 0:rows, 128 * q:128 * q + 128] = jnp.where(hit, 1.0, 0.0).astype(BF16)

    def to_quadrants(lhs, g):
        total = None
        for k, (t, gg) in enumerate(PAIRS):
            if gg == g:
                rows = 16 if t == 5 else 256
                term = jnp.dot(lhs(256 * t, rows), pick[k, 0:rows, :], preferred_element_type=F32)
                total = term if total is None else total + term
        return total

    table = gain_ref[...]
    high = table.astype(BF16).astype(F32)
    mid = (table - high).astype(BF16).astype(F32)
    low = table - high - mid
    thirds = jnp.concatenate([high, mid, low, jnp.zeros_like(low)], axis=0).astype(BF16)
    for g in range(3):
        total = to_quadrants(lambda at_, n: thirds[:, at_:at_ + n], g)
        for q in range(4):
            third = total[:, 128 * q:128 * q + 128]
            gain_rows[3 * q + g] = third[0:8] + third[8:16] + third[16:24]

    for copy in loads:
        copy.wait()
    for m in range(2):
        def columns(k, _, m=m):
            rows = pl.ds(pl.multiple_of(144 * k, 16), 144)
            for g in range(3):
                total = to_quadrants(lambda at_, n: natural[m, rows, at_:at_ + n], g).astype(BF16)
                for q in range(4):
                    turned[3 * q + g, rows, 128 * m:128 * m + 128] = total[:, 128 * q:128 * q + 128]
            return 0
        lax.fori_loop(0, 9, columns, 0)

    for k, ds in ((0, -1), (1, 1)):
        @pl.when(there(0, ds))
        def _():
            mask_copy(ds, incoming=True).wait_recv()
            mask_copy(ds).wait_send()
            tile[16 * k:16 * k + 8, :] = mask_land[k]

        @pl.when(jnp.logical_not(there(0, ds)))
        def _():
            tile[16 * k:16 * k + 8, :] = jnp.zeros((8, 128), F32)
    tile[8:16, :] = mask_own[...]
    tile[24:32, :] = class_ref[...].astype(F32)
    tile[32:128, :] = jnp.zeros((96, 128), F32)
    strip[0:8, :] = jnp.zeros((8, 128), F32)
    strip[136:152, :] = jnp.zeros((16, 128), F32)
    strip[8:136, :] = tile[...].T
    near = strip[pl.ds(pl.multiple_of(16 * c, 16), 32), :]
    for j in range(16):
        mask[j] = jnp.broadcast_to(near[:, j + 4:j + 5], (32, 128))
    for j in range(8):
        kind[16 * j:16 * j + 16, :] = jnp.broadcast_to(near[8:24, 24 + j:25 + j], (16, 128))

    def fill(qg, _):
        which = kind[...]
        value = jnp.zeros((128, 128), F32)
        for k in range(CLASSES):
            value = jnp.where(which == float(k), gain_rows[qg, k:k + 1, :], value)
        gains[qg] = value
        return 0
    lax.fori_loop(0, 12, fill, 0)

    def heading(q):
        return (1 if LOWX[q] else -1), (1 if LOWY[q] else -1)

    def edge(q, kind):
        dx, dy = heading(q)
        return ((0, dy), (dx, 0), (dx, dy))[kind]

    def edge_copy(p, q, kind):
        dc, ds = edge(q, kind)
        groups = pl.ds(3 * q, 3)
        if kind == 0:
            src = e0.at[groups, pl.ds(8 if LOWY[q] else 0, 4), pl.ds(off_i(q), 16)]
            dst = yl.at[p, groups]
        elif kind == 1:
            src, dst = xs.at[groups], xl.at[p, groups]
        else:
            src, dst = cs.at[groups], cl.at[p, groups]
        return pltpu.make_async_remote_copy(
            src_ref=src, dst_ref=dst, send_sem=h_send.at[p, q, kind], recv_sem=h_recv.at[p, q, kind],
            device_id=at(dc, ds), device_id_type=MESH)

    def corner(q, landed):
        for d, (n, at_) in enumerate(((3, 0), (2, 3), (1, 5))):
            j = (3 - d if landed else 11 - d) if LOWY[q] else (8 + d if landed else d)
            i = ((8 if landed else 24) - n) if LOWX[q] else (16 if landed else 0)
            yield n, at_, j, i

    def send_edges(p, q):
        i = 20 if LOWX[q] else 0

        def pack(g, _):
            qg = 3 * q + g
            for j in range(8):
                xs[qg, j // 2, 4 * (j % 2):4 * (j % 2) + 4, :] = e0[qg, off_j(q) + j, i:i + 4, :]
            for n, at_, j, ii in corner(q, False):
                cs[qg, at_:at_ + n, :] = e0[qg, j, ii:ii + n, :]
            return 0
        lax.fori_loop(0, 3, pack, 0, unroll=3)
        for kind in range(3):
            @pl.when(there(*edge(q, kind)))
            def _():
                edge_copy(p, q, kind).start()

    def take_edges(p, q):
        i = 4 if LOWX[q] else 16
        jh = 0 if LOWY[q] else 8
        for kind in range(3):
            dc, ds = edge(q, kind)

            @pl.when(there(dc, ds))
            def _():
                edge_copy(p, q, kind).wait_send()

            @pl.when(there(-dc, -ds))
            def _():
                edge_copy(p, q, kind).wait_recv()

                def unpack(g, _):
                    qg = 3 * q + g
                    if kind == 0:
                        e0[qg, jh:jh + 4, off_i(q):off_i(q) + 16, :] = yl[p, qg]
                    elif kind == 1:
                        for j in range(8):
                            e0[qg, off_j(q) + j, i:i + 4, :] = xl[p, qg, j // 2, 4 * (j % 2):4 * (j % 2) + 4, :]
                    else:
                        for n, at_, j, ii in corner(q, True):
                            e0[qg, j, ii:ii + n, :] = cl[p, qg, at_:at_ + n, :]
                    return 0
                lax.fori_loop(0, 3, unpack, 0, unroll=3)

    def substep(q, t):
        src, dst = (e0, e1) if t % 2 == 0 else (e1, e0)
        if LOWY[q]:
            j0, n, jm = t + 1, 11 - t, 0
        else:
            j0, n, jm = 0, 11 - t, 4
        if LOWX[q]:
            di, im, starts = -1, 0, (8, 16) + (() if t == 3 else (1,))
        else:
            di, im, starts = 1, 8, (0, 8) + (() if t == 3 else (15,))

        groups = slice(3 * q, 3 * q + 3)
        c0, cx, cy = (coef[k, groups, :].reshape(3, 1, 1, 128) for k in range(3))
        for i in starts:
            for first in range(j0, j0 + n, 4):
                m = min(4, j0 + n - first)
                if LOWY[q]:
                    both = src[groups, first - 1:first + m, i:i + 8, :]
                    mid, across = both[:, 1:], both[:, :-1]
                else:
                    both = src[groups, first:first + m + 1, i:i + 8, :]
                    mid, across = both[:, :-1], both[:, 1:]
                along = src[groups, first:first + m, i + di:i + di + 8, :]
                sea = mask[first + jm:first + jm + m, i + im:i + im + 8, :][None]
                dst[groups, first:first + m, i:i + 8, :] = (c0 * mid + cx * along + cy * across) * sea

    def interior(q):
        return slice(off_j(q), off_j(q) + 8), slice(off_i(q), off_i(q) + 16)

    def place(qg):
        q = (qg >= 3).astype(I32) + (qg >= 6).astype(I32) + (qg >= 9).astype(I32)
        j = jnp.where(jnp.logical_or(q == 0, q == 2), 4, 0)
        i = pl.multiple_of(jnp.where(jnp.logical_or(q == 0, q == 3), 8, 0), 8)
        return pl.ds(j, 8), pl.ds(i, 16)

    def narrow(q):
        js, is_ = interior(q)
        for g in range(3):
            qg = 3 * q + g
            xb[:, 128 * qg:128 * qg + 128] = e0[qg, js, is_, :].reshape(128, 128).astype(BF16)

    def first_half(qg, _):
        part[qg] = jnp.dot(xb[:, :768], weights[qg, :768, :], preferred_element_type=F32)
        return 0

    def second_half(qg, _):
        got = part[qg] + jnp.dot(xb[:, 768:], weights[qg, 768:, :], preferred_element_type=F32)
        change = gains[qg] * got[:, :128] + got[:, 128:]
        slope[qg] = change
        js, is_ = place(qg)
        state = e0[qg, js, is_, :].reshape(128, 128)
        yb[:, pl.ds(pl.multiple_of(128 * qg, 128), 128)] = (state + change).astype(BF16)
        return 0

    def finish(q):
        js, is_ = interior(q)

        def body(g, _):
            qg = 3 * q + g
            got = jnp.dot(yb[...], weights[qg], preferred_element_type=F32)
            change = gains[qg] * got[:, :128] + got[:, 128:]
            state = e0[qg, js, is_, :].reshape(128, 128)
            e0[qg, js, is_, :] = (state + 0.5 * (slope[qg] + change)).reshape(8, 16, 128)
            return 0
        lax.fori_loop(0, 3, body, 0, unroll=3)

    own_a.wait()
    for k in range(1, NSPEC):
        a_copy(k, incoming=True).wait_recv()
    for q in range(4):
        for g in range(3):
            pieces = []
            for rr in range(NSPEC):
                a, b = max(SLOT * rr, 128 * g) - SLOT * rr, min(SLOT * rr + SLOT, 128 * g + 128) - SLOT * rr
                if a >= b:
                    continue
                rel = relative(q, rr)
                cut = min(b, KEPT[rel])
                if a < cut:
                    pieces.append(land_a[rr, BASE[rel] + a:BASE[rel] + cut, :])
                if cut < b:
                    pieces.append(jnp.zeros((b - max(a, cut), 128), F32))
            e0[3 * q + g, off_j(q):off_j(q) + 8, off_i(q):off_i(q) + 16, :] = (
                jnp.concatenate(pieces, axis=0).T.reshape(8, 16, 128))
        send_edges(0, q)

    for rr in range(NSPEC):
        blocks = []
        for q in range(4):
            spot = lax.broadcasted_iota(I32, (SLOT, 176), 0)
            want = local_bin(jnp.full((SLOT, 176), relative(q, rr), I32), spot) + 2 * rr
            hit = lax.broadcasted_iota(I32, (SLOT, 176), 1) == want
            blocks.append(jnp.where(hit, 1.0, 0.0).astype(BF16))
        onehot = jnp.concatenate(blocks, axis=0)

        def lines(qg, _, rr=rr, onehot=onehot):
            got = jnp.dot(onehot, turned[qg, 160 * rr:160 * rr + 176, :], preferred_element_type=F32).astype(BF16)
            for q in range(4):
                weights[qg, 384 * q + SLOT * rr:384 * q + SLOT * rr + SLOT, :] = got[SLOT * q:SLOT * q + SLOT]
            return 0
        lax.fori_loop(0, 12, lines, 0, unroll=2)

    def phase(p, _):
        for q in range(4):
            take_edges(p, q)

            @pl.when(p > 0)
            def _():
                substep(q, 0)
                substep(q, 1)
            substep(q, 2)
            substep(q, 3)
            narrow(q)
            if q == 1:
                lax.fori_loop(0, 12, first_half, 0, unroll=4)
        lax.fori_loop(0, 12, second_half, 0, unroll=4)
        for q in range(4):
            finish(q)
            send_edges(p + 1, q)
        return 0

    lax.fori_loop(0, ITERS, phase, 0)

    for k in range(1, NSPEC):
        a_copy(k).wait_send()

    def b_copy(k, q, odd, incoming=False):
        peer = lax.rem(r + k, NSPEC)
        slot = block_of(peer, half) if incoming else c
        rel = relative(q, odd)
        rows = pl.ds(BASE[rel], KEPT[rel])
        return pltpu.make_async_remote_copy(
            src_ref=send_a.at[peer, rows], dst_ref=land_b.at[slot, rows],
            send_sem=b_send.at[k, q], recv_sem=b_recv.at[slot, rel], device_id=(s, peer), device_id_type=MESH)

    for q in range(4):
        take_edges(ITERS, q)
        substep(q, 2)
        substep(q, 3)
        js, is_ = interior(q)
        for g in range(3):
            block = e0[3 * q + g, js, is_, :].reshape(128, 128).T
            for rr in range(NSPEC):
                a, b = max(SLOT * rr, 128 * g), min(SLOT * rr + SLOT, 128 * g + 128)
                rel = relative(q, rr)
                b = min(b, SLOT * rr + KEPT[rel])
                if a < b:
                    send_a[rr, BASE[rel] + a - SLOT * rr:BASE[rel] + b - SLOT * rr, :] = block[a - 128 * g:b - 128 * g]
        for k in range(1, NSPEC):
            for odd in range(2):
                @pl.when(lax.rem(r + k, 2) == odd)
                def _():
                    b_copy(k, q, odd).start()
    own_b = pltpu.make_async_copy(send_a.at[r], land_b.at[c], a_send.at[0])
    own_b.start()
    own_b.wait()
    for k in range(1, NSPEC):
        for q in range(4):
            for odd in range(2):
                @pl.when(lax.rem(r, 2) == odd)
                def _():
                    b_copy(k, q, odd, incoming=True).wait_recv()
    for rel in range(4):
        for f in range(FULL[rel]):
            rows = slice(BASE[rel] + 8 * f, BASE[rel] + 8 * f + 8)
            parts = swap_blocks([land_b[cc, rows, :] for cc in range(8)])
            for j in range(8):
                out_ref[pl.ds((36 * f + 9 * rel) * 8 + j, 8, stride=8), :] = parts[j]
        n = FULL[rel]
        parts = swap_blocks([land_b[cc, BASE[rel] + 8 * n:BASE[rel] + 9 * n, :] for cc in range(8)])
        for j in range(8):
            out_ref[pl.ds((9 * rel + 8) * 8 + j, n, stride=288), :] = parts[j]
    for k in range(1, NSPEC):
        for q in range(4):
            for odd in range(2):
                @pl.when(lax.rem(r + k, 2) == odd)
                def _():
                    b_copy(k, q, odd).wait_send()


def shards(ns, spectrum, ocean_mask, depth_class, freq_speed, coupling, source, gain_table):
    vmem, hbm = pl.BlockSpec(memory_space=pltpu.VMEM), pl.BlockSpec(memory_space=pl.ANY)
    dma = pltpu.SemaphoreType.DMA
    out = pl.pallas_call(
        functools.partial(kernel, ns),
        out_shape=jax.ShapeDtypeStruct((LOCAL * 8, 128), F32),
        in_specs=[vmem, vmem, vmem, pl.BlockSpec(memory_space=pltpu.SMEM), hbm, hbm, vmem],
        out_specs=vmem,
        scratch_shapes=[
            pltpu.VMEM((2, BINS, BINS), BF16),
            pltpu.VMEM((12, BINS, 256), BF16),
            pltpu.VMEM((12, 1536, 256), BF16),
            pltpu.VMEM((8, 256, 512), BF16),
            pltpu.VMEM((12, 12, 24, 128), F32),
            pltpu.VMEM((12, 12, 24, 128), F32),
            pltpu.VMEM((12, 128, 128), F32),
            pltpu.VMEM((12, 128, 256), F32),
            pltpu.VMEM((128, 1536), BF16),
            pltpu.VMEM((128, 1536), BF16),
            pltpu.VMEM((12, 128, 128), F32),
            pltpu.VMEM((12, 8, 128), F32),
            pltpu.VMEM((16, 32, 128), F32),
            pltpu.VMEM((3, 16, 128), F32),
            pltpu.VMEM((8, ROWS, 128), F32),
            pltpu.VMEM((8, ROWS, 128), F32),
            pltpu.VMEM((8, ROWS, 128), F32),
            pltpu.VMEM((12, 4, 8, 128), F32),
            pltpu.VMEM((12, 8, 128), F32),
            pltpu.VMEM((PHASES, 12, 4, 16, 128), F32),
            pltpu.VMEM((PHASES, 12, 4, 8, 128), F32),
            pltpu.VMEM((PHASES, 12, 8, 128), F32),
            pltpu.VMEM((128, 128), F32),
            pltpu.VMEM((152, 128), F32),
            pltpu.VMEM((128, 128), F32),
            pltpu.VMEM((8, 128), F32),
            pltpu.VMEM((2, 8, 128), F32),
            dma((2,)), dma((8,)), dma((8,)), dma((8, 4)), dma((8, 4)),
            dma((PHASES, 4, 3)), dma((PHASES, 4, 3)), dma((2,)), dma((2,)),
        ],
        compiler_params=pltpu.CompilerParams(
            collective_id=0, has_side_effects=True, vmem_limit_bytes=56 * 2**20),
        cost_estimate=pl.CostEstimate(flops=12 * 10**9, bytes_accessed=9 * 10**6, transcendentals=0),
        name="wave_steps",
    )(spectrum.reshape(LOCAL * 8, 128), ocean_mask, depth_class, freq_speed, coupling, source, gain_table)
    return out.reshape(LOCAL, 8, 128)


def solution(mesh):
    placed = (P("spec", "space", None), P("space", None), P("space", None), P(), P(), P(), P())
    return jax.shard_map(
        functools.partial(shards, mesh.shape["space"]), mesh=mesh, in_specs=placed,
        out_specs=P("spec", "space", None), check_vma=False)
```

```python
import functools
import math

import jax
import jax.numpy as jnp
from jax import lax
from jax.experimental import pallas as pl
from jax.experimental.pallas import tpu as pltpu
from jax.sharding import PartitionSpec as P

MESH = pl.DeviceIdType.MESH
F32, BF16, I32 = jnp.float32, jnp.bfloat16, jnp.int32
BINS, NDIR, NFREQ, CLASSES = 1296, 36, 36, 8
ITERS = 4
NSPEC, LOCAL = 8, 162
SLOT = 48
FULL = (5, 5, 4, 4)
BASE = (0, 48, 96, 136)
KEPT = (48, 48, 40, 40)
LIVE = (45, 45, 36, 36)
ROWS = 176
QUADS = (0, 2, 1, 3)
LOWX, LOWY = (True, False, False, True), (True, False, True, False)
PAIRS = ((0, 0), (1, 0), (1, 1), (2, 1), (3, 1), (3, 2), (4, 2), (5, 2))
PHASES = ITERS + 1


def off_j(q):
    return 4 if LOWY[q] else 0


def off_i(q):
    return 8 if LOWX[q] else 0


def block_of(r, half):
    low = lax.rem(r // 4 + half, 2)
    x = lax.rem(r, 4)
    return jnp.where(low == 0, x, 7 - x)


def owner_of(c, half):
    x = jnp.where(c < 4, c, 7 - c)
    return lax.rem(c // 4 + half, 2) * 4 + x


def swap_blocks(parts):
    lane = lax.broadcasted_iota(I32, parts[0].shape, 1)
    for h in (4, 2, 1):
        keep = (lane & (16 * h)) == 0
        new = list(parts)
        for j in range(8):
            if j & h == 0:
                a, b = parts[j], parts[j + h]
                new[j] = jnp.where(keep, a, pltpu.roll(b, 16 * h, 1))
                new[j + h] = jnp.where(keep, pltpu.roll(a, 128 - 16 * h, 1), b)
        parts = new
    return parts


def local_bin(rel, idx):
    many = rel < 2
    whole = jnp.where(many, 40, 32)
    runs = jnp.where(many, 5, 4)
    first = 36 * (idx >> 3) + (idx & 7)
    last = 36 * (idx - whole) + 8
    return jnp.where(idx < whole, first + 9 * rel, jnp.where(idx < whole + runs, last + 9 * rel, -10000))


def places(q, g, shape):
    slot = 128 * g + lax.broadcasted_iota(I32, shape, len(shape) - 1)
    r = jnp.zeros_like(slot)
    for k in range(1, 8):
        r = r + (slot >= SLOT * k).astype(I32)
    return r, q ^ (2 * (r & 1)), slot - SLOT * r


def relative(q, r):
    return QUADS[q] ^ (2 * (r & 1))


def kernel(ns, x_ref, mask_ref, class_ref, speed_ref, coupling_ref, source_ref, gain_ref, out_ref,
           natural, turned, weights, pick, lift, e0, e1, slope, part, xb, yb, gains, gain_rows, mask, coef,
           send_a, land_a, land_b, xs, cs, yl, xl, cl, tile, strip, kind, mask_own, mask_land,
           w_sem, a_send, a_recv, b_send, b_recv, own_sem, h_send, h_recv, m_send, m_recv):
    r = lax.axis_index("spec")
    s = lax.axis_index("space")
    half = s // (ns // 2)
    c = block_of(r, half)

    def at(dc, ds):
        cc, ss = jnp.clip(c + dc, 0, NSPEC - 1), jnp.clip(s + ds, 0, ns - 1)
        return (ss, owner_of(cc, ss // (ns // 2)))

    def there(dc, ds):
        ok = None
        for cond in ([c + dc >= 0, c + dc < NSPEC] if dc else []) + ([s + ds >= 0, s + ds < ns] if ds else []):
            ok = cond if ok is None else jnp.logical_and(ok, cond)
        return ok

    loads = [pltpu.make_async_copy(ref, natural.at[m], w_sem.at[m]) for m, ref in enumerate((coupling_ref, source_ref))]
    for copy in loads:
        copy.start()
    for slot in range(NSPEC):
        for rel in range(4):
            end = BASE[rel] + KEPT[rel]
            land_a[slot, end - 8:end, :] = jnp.zeros((8, 128), F32)
    barrier = pltpu.get_barrier_semaphore()
    around = [(dc, ds) for ds in (-1, 1) for dc in (-1, 0, 1)]
    for k in range(1, NSPEC):
        pl.semaphore_signal(barrier, inc=1, device_id=(s, lax.rem(r + k, NSPEC)), device_id_type=MESH)
    for dc, ds in around:
        @pl.when(there(dc, ds))
        def _():
            pl.semaphore_signal(barrier, inc=1, device_id=at(dc, ds), device_id_type=MESH)

    mask_own[...] = mask_ref[...].astype(F32)

    for rel in range(4):
        for f in range(FULL[rel]):
            parts = [x_ref[pl.ds((36 * f + 9 * rel) * 8 + j, 8, stride=8), :] for j in range(8)]
            for cc, block in enumerate(swap_blocks(parts)):
                send_a[cc, BASE[rel] + 8 * f:BASE[rel] + 8 * f + 8, :] = block
        n = FULL[rel]
        parts = [x_ref[pl.ds((9 * rel + 8) * 8 + j, n, stride=288), :] for j in range(8)]
        for cc, block in enumerate(swap_blocks(parts)):
            send_a[cc, BASE[rel] + 8 * n:BASE[rel] + 8 * n + 8, :] = jnp.zeros((8, 128), F32)
            send_a[cc, BASE[rel] + 8 * n:BASE[rel] + 9 * n, :] = block

    beside = (c > 0).astype(I32) + (c < NSPEC - 1).astype(I32)
    beyond = (s > 0).astype(I32) + (s < ns - 1).astype(I32)
    pl.semaphore_wait(barrier, NSPEC - 1 + beyond * (1 + beside))

    def a_copy(k, rel, incoming=False):
        peer = lax.rem(r + k, NSPEC)
        slot = peer if incoming else r
        rows = pl.ds(BASE[rel], LIVE[rel])
        return pltpu.make_async_remote_copy(
            src_ref=send_a.at[block_of(peer, half), rows], dst_ref=land_a.at[slot, rows],
            send_sem=a_send.at[k, rel], recv_sem=a_recv.at[slot, rel], device_id=(s, peer), device_id_type=MESH)

    for rel in range(4):
        for k in range(1, NSPEC):
            a_copy(k, rel).start()
    own_a = pltpu.make_async_copy(send_a.at[c], land_a.at[r], own_sem)
    own_a.start()

    def mask_copy(ds, incoming=False):
        k = (1 if ds < 0 else 0) if not incoming else (0 if ds < 0 else 1)
        return pltpu.make_async_remote_copy(
            src_ref=mask_own, dst_ref=mask_land.at[k], send_sem=m_send.at[k], recv_sem=m_recv.at[k],
            device_id=at(0, ds), device_id_type=MESH)

    for ds in (-1, 1):
        @pl.when(there(0, ds))
        def _():
            mask_copy(ds).start()

    def clear(qg, _):
        e0[qg] = jnp.zeros((12, 24, 128), F32)
        e1[qg] = jnp.zeros((12, 24, 128), F32)
        return 0
    lax.fori_loop(0, 12, clear, 0)

    row = lax.broadcasted_iota(I32, (16, 128), 0)
    quad = (row >= 3).astype(I32) + (row >= 6).astype(I32) + (row >= 9).astype(I32)
    group = row - 3 * quad
    quad = jnp.where(quad == 1, 2, jnp.where(quad == 2, 1, quad))
    home, rel, idx = places(quad, group, (16, 128))
    here = local_bin(rel, idx)
    many = rel < 2
    whole = jnp.where(many, 40, 32)
    run = jnp.where(idx < whole, idx >> 3, idx - whole)
    step = jnp.where(idx < whole, idx & 7, 8)
    freq = ((9 * home) >> 1) + run + jnp.where(many, 0, home & 1)
    group_speed = jnp.zeros((16, 128), F32)
    for k in range(NFREQ):
        group_speed = jnp.where(freq == k, speed_ref[k], group_speed)
    group_speed = jnp.where(here >= 0, group_speed, 0.0)
    cosine, sine = jnp.zeros((16, 128), F32), jnp.zeros((16, 128), F32)
    for k in range(9):
        cosine = jnp.where(step == k, math.cos(2.0 * math.pi * (k + 0.5) / NDIR), cosine)
        sine = jnp.where(step == k, math.sin(2.0 * math.pi * (k + 0.5) / NDIR), sine)
    even = (quad & 1) == 0
    ax = group_speed * jnp.where(even, cosine, sine)
    ay = group_speed * jnp.where(even, sine, cosine)
    coef[0] = 1.0 - ax - ay
    coef[1] = ax
    coef[2] = ay

    for k, (t, g) in enumerate(PAIRS):
        rows = 16 if t == 5 else 256
        for q in range(4):
            home, rel, idx = places(jnp.full((1, 128), QUADS[q], I32), g, (1, 128))
            want = LOCAL * home + local_bin(rel, idx) - 256 * t
            hit = lax.broadcasted_iota(I32, (rows, 128), 0) == want
            pick[256 * k:256 * k + rows, 128 * q:128 * q + 128] = jnp.where(hit, 1.0, 0.0).astype(BF16)

    def to_quadrants(lhs, g):
        first, start, depth = ((0, 0, 512), (2, 256, 768), (5, 768, 528))[g]
        return jnp.dot(lhs(start, depth), pick[256 * first:256 * first + depth, :], preferred_element_type=F32)

    for rr in range(NSPEC):
        for q in range(4):
            spot = lax.broadcasted_iota(I32, (SLOT, 176), 0)
            want = local_bin(jnp.full((SLOT, 176), relative(q, rr), I32), spot) + 2 * rr
            hit = lax.broadcasted_iota(I32, (SLOT, 176), 1) == want
            lift[rr, SLOT * q:SLOT * q + SLOT, :] = jnp.where(hit, 1.0, 0.0).astype(BF16)

    table = gain_ref[...]
    high = table.astype(BF16).astype(F32)
    mid = (table - high).astype(BF16).astype(F32)
    low = table - high - mid
    thirds = jnp.concatenate([high, mid, low, jnp.zeros_like(low)], axis=0).astype(BF16)
    for g in range(3):
        total = to_quadrants(lambda at_, n: thirds[:, at_:at_ + n], g)
        for q in range(4):
            third = total[:, 128 * q:128 * q + 128]
            gain_rows[3 * q + g] = third[0:8] + third[8:16] + third[16:24]

    for copy in loads:
        copy.wait()
    for m in range(2):
        def columns(k, _, m=m):
            rows = pl.ds(pl.multiple_of(432 * k, 16), 432)
            for g in range(3):
                total = to_quadrants(lambda at_, n: natural[m, rows, at_:at_ + n], g).astype(BF16)
                for q in range(4):
                    turned[3 * q + g, rows, 128 * m:128 * m + 128] = total[:, 128 * q:128 * q + 128]
            return 0
        lax.fori_loop(0, 3, columns, 0)

    for k, ds in ((0, -1), (1, 1)):
        @pl.when(there(0, ds))
        def _():
            mask_copy(ds, incoming=True).wait_recv()
            mask_copy(ds).wait_send()
            tile[16 * k:16 * k + 8, :] = mask_land[k]

        @pl.when(jnp.logical_not(there(0, ds)))
        def _():
            tile[16 * k:16 * k + 8, :] = jnp.zeros((8, 128), F32)
    tile[8:16, :] = mask_own[...]
    tile[24:32, :] = class_ref[...].astype(F32)
    tile[32:128, :] = jnp.zeros((96, 128), F32)
    strip[0:8, :] = jnp.zeros((8, 128), F32)
    strip[136:152, :] = jnp.zeros((16, 128), F32)
    strip[8:136, :] = tile[...].T
    near = strip[pl.ds(pl.multiple_of(16 * c, 16), 32), :]
    for j in range(16):
        mask[j] = jnp.broadcast_to(near[:, j + 4:j + 5], (32, 128))
    for j in range(8):
        kind[16 * j:16 * j + 16, :] = jnp.broadcast_to(near[8:24, 24 + j:25 + j], (16, 128))

    def fill(qg, _):
        which = kind[...]
        value = jnp.zeros((128, 128), F32)
        for k in range(CLASSES):
            value = jnp.where(which == float(k), gain_rows[qg, k:k + 1, :], value)
        gains[qg] = value
        return 0
    lax.fori_loop(0, 12, fill, 0)

    def heading(q):
        return (1 if LOWX[q] else -1), (1 if LOWY[q] else -1)

    def edge(q, kind):
        dx, dy = heading(q)
        return ((0, dy), (dx, 0), (dx, dy))[kind]

    def edge_copy(p, q, kind):
        dc, ds = edge(q, kind)
        groups = pl.ds(3 * q, 3)
        if kind == 0:
            src = e0.at[groups, pl.ds(8 if LOWY[q] else 0, 4), pl.ds(off_i(q), 16)]
            dst = yl.at[p, groups]
        elif kind == 1:
            src, dst = xs.at[groups], xl.at[p, groups]
        else:
            src, dst = cs.at[groups], cl.at[p, groups]
        return pltpu.make_async_remote_copy(
            src_ref=src, dst_ref=dst, send_sem=h_send.at[p, q, kind], recv_sem=h_recv.at[p, q, kind],
            device_id=at(dc, ds), device_id_type=MESH)

    def corner(q, landed):
        for d, (n, at_) in enumerate(((3, 0), (2, 3), (1, 5))):
            j = (3 - d if landed else 11 - d) if LOWY[q] else (8 + d if landed else d)
            i = ((8 if landed else 24) - n) if LOWX[q] else (16 if landed else 0)
            yield n, at_, j, i

    def send_edges(p, q):
        i = 20 if LOWX[q] else 0

        def pack(g, _):
            qg = 3 * q + g
            for j in range(8):
                xs[qg, j // 2, 4 * (j % 2):4 * (j % 2) + 4, :] = e0[qg, off_j(q) + j, i:i + 4, :]
            for n, at_, j, ii in corner(q, False):
                cs[qg, at_:at_ + n, :] = e0[qg, j, ii:ii + n, :]
            return 0
        lax.fori_loop(0, 3, pack, 0, unroll=3)
        for kind in range(3):
            @pl.when(there(*edge(q, kind)))
            def _():
                edge_copy(p, q, kind).start()

    def take_edges(p, q):
        i = 4 if LOWX[q] else 16
        jh = 0 if LOWY[q] else 8
        for kind in range(3):
            dc, ds = edge(q, kind)

            @pl.when(there(dc, ds))
            def _():
                edge_copy(p, q, kind).wait_send()

            @pl.when(there(-dc, -ds))
            def _():
                edge_copy(p, q, kind).wait_recv()

                def unpack(g, _):
                    qg = 3 * q + g
                    if kind == 0:
                        e0[qg, jh:jh + 4, off_i(q):off_i(q) + 16, :] = yl[p, qg]
                    elif kind == 1:
                        for j in range(8):
                            e0[qg, off_j(q) + j, i:i + 4, :] = xl[p, qg, j // 2, 4 * (j % 2):4 * (j % 2) + 4, :]
                    else:
                        for n, at_, j, ii in corner(q, True):
                            e0[qg, j, ii:ii + n, :] = cl[p, qg, at_:at_ + n, :]
                    return 0
                lax.fori_loop(0, 3, unpack, 0, unroll=3)

    def substep(q, t):
        src, dst = (e0, e1) if t % 2 == 0 else (e1, e0)
        if LOWY[q]:
            j0, n, jm = t + 1, 11 - t, 0
        else:
            j0, n, jm = 0, 11 - t, 4
        if LOWX[q]:
            di, im, starts = -1, 0, (8, 16) + (() if t == 3 else (1,))
        else:
            di, im, starts = 1, 8, (0, 8) + (() if t == 3 else (15,))

        groups = slice(3 * q, 3 * q + 3)
        c0, cx, cy = (coef[k, groups, :].reshape(3, 1, 1, 128) for k in range(3))
        for i in starts:
            for first in range(j0, j0 + n, 4):
                m = min(4, j0 + n - first)
                if LOWY[q]:
                    both = src[groups, first - 1:first + m, i:i + 8, :]
                    mid, across = both[:, 1:], both[:, :-1]
                else:
                    both = src[groups, first:first + m + 1, i:i + 8, :]
                    mid, across = both[:, :-1], both[:, 1:]
                along = src[groups, first:first + m, i + di:i + di + 8, :]
                sea = mask[first + jm:first + jm + m, i + im:i + im + 8, :][None]
                dst[groups, first:first + m, i:i + 8, :] = (c0 * mid + cx * along + cy * across) * sea

    def interior(q):
        return slice(off_j(q), off_j(q) + 8), slice(off_i(q), off_i(q) + 16)

    def narrow(q):
        js, is_ = interior(q)
        for g in range(3):
            qg = 3 * q + g
            xb[:, 128 * qg:128 * qg + 128] = e0[qg, js, is_, :].reshape(128, 128).astype(BF16)

    def first_half(qg):
        part[qg] = jnp.dot(xb[:, :768], weights[qg, :768, :], preferred_element_type=F32)

    def second_half(qg):
        got = part[qg] + jnp.dot(xb[:, 768:], weights[qg, 768:, :], preferred_element_type=F32)
        change = gains[qg] * got[:, :128] + got[:, 128:]
        slope[qg] = change
        js, is_ = interior(qg // 3)
        state = e0[qg, js, is_, :].reshape(128, 128)
        yb[:, 128 * qg:128 * qg + 128] = (state + change).astype(BF16)

    def finish(q):
        js, is_ = interior(q)

        for qg in range(3 * q, 3 * q + 3):
            got = jnp.dot(yb[...], weights[qg], preferred_element_type=F32)
            change = gains[qg] * got[:, :128] + got[:, 128:]
            state = e0[qg, js, is_, :].reshape(128, 128)
            e0[qg, js, is_, :] = (state + 0.5 * (slope[qg] + change)).reshape(8, 16, 128)

    own_a.wait()
    for rel in range(4):
        for k in range(1, NSPEC):
            a_copy(k, rel, incoming=True).wait_recv()
    for q in range(4):
        for g in range(3):
            pieces = []
            for rr in range(NSPEC):
                a, b = max(SLOT * rr, 128 * g) - SLOT * rr, min(SLOT * rr + SLOT, 128 * g + 128) - SLOT * rr
                if a >= b:
                    continue
                rel = relative(q, rr)
                cut = min(b, KEPT[rel])
                if a < cut:
                    pieces.append(land_a[rr, BASE[rel] + a:BASE[rel] + cut, :])
                if cut < b:
                    pieces.append(jnp.zeros((b - max(a, cut), 128), F32))
            e0[3 * q + g, off_j(q):off_j(q) + 8, off_i(q):off_i(q) + 16, :] = (
                jnp.concatenate(pieces, axis=0).T.reshape(8, 16, 128))
        send_edges(0, q)

    def lines(qg, _):
        for rr in range(NSPEC):
            got = jnp.dot(lift[rr], turned[qg, 160 * rr:160 * rr + 176, :], preferred_element_type=F32).astype(BF16)
            for q in range(4):
                weights[qg, 384 * q + SLOT * rr:384 * q + SLOT * rr + SLOT, :] = got[SLOT * q:SLOT * q + SLOT]
        return 0
    lax.fori_loop(0, 12, lines, 0)

    def phase(p, _):
        for q in range(4):
            take_edges(p, q)

            @pl.when(p > 0)
            def _():
                substep(q, 0)
                substep(q, 1)
            substep(q, 2)
            substep(q, 3)
            narrow(q)
            if q == 1:
                for qg in range(12):
                    first_half(qg)
        for qg in range(12):
            second_half(qg)
        for q in range(4):
            finish(q)
            send_edges(p + 1, q)
        return 0

    lax.fori_loop(0, ITERS, phase, 0)

    for rel in range(4):
        for k in range(1, NSPEC):
            a_copy(k, rel).wait_send()

    def b_copy(k, q, odd, incoming=False):
        peer = lax.rem(r + k, NSPEC)
        slot = block_of(peer, half) if incoming else c
        rel = relative(q, odd)
        rows = pl.ds(BASE[rel], LIVE[rel])
        return pltpu.make_async_remote_copy(
            src_ref=send_a.at[peer, rows], dst_ref=land_b.at[slot, rows],
            send_sem=b_send.at[k, q], recv_sem=b_recv.at[slot, rel], device_id=(s, peer), device_id_type=MESH)

    for q in range(4):
        take_edges(ITERS, q)
        substep(q, 2)
        substep(q, 3)
        js, is_ = interior(q)
        for g in range(3):
            block = e0[3 * q + g, js, is_, :].reshape(128, 128).T
            for rr in range(NSPEC):
                a, b = max(SLOT * rr, 128 * g), min(SLOT * rr + SLOT, 128 * g + 128)
                rel = relative(q, rr)
                b = min(b, SLOT * rr + KEPT[rel])
                if a < b:
                    send_a[rr, BASE[rel] + a - SLOT * rr:BASE[rel] + b - SLOT * rr, :] = block[a - 128 * g:b - 128 * g]
        for k in range(1, NSPEC):
            for odd in range(2):
                @pl.when(lax.rem(r + k, 2) == odd)
                def _():
                    b_copy(k, q, odd).start()
    own_b = pltpu.make_async_copy(send_a.at[r], land_b.at[c], own_sem)
    own_b.start()

    def put(rel):
        n = FULL[rel]
        for f in range(n):
            rows = slice(BASE[rel] + 8 * f, BASE[rel] + 8 * f + 8)
            parts = swap_blocks([land_b[cc, rows, :] for cc in range(8)])
            for j in range(8):
                out_ref[pl.ds((36 * f + 9 * rel) * 8 + j, 8, stride=8), :] = parts[j]
        parts = swap_blocks([land_b[cc, BASE[rel] + 8 * n:BASE[rel] + 9 * n, :] for cc in range(8)])
        for j in range(8):
            out_ref[pl.ds((9 * rel + 8) * 8 + j, n, stride=288), :] = parts[j]

    own_b.wait()
    for odd in range(2):
        @pl.when(lax.rem(r, 2) == odd)
        def _():
            for q in range(4):
                for k in range(1, NSPEC):
                    b_copy(k, q, odd, incoming=True).wait_recv()
                put(relative(q, odd))
    for k in range(1, NSPEC):
        for q in range(4):
            for odd in range(2):
                @pl.when(lax.rem(r + k, 2) == odd)
                def _():
                    b_copy(k, q, odd).wait_send()


def shards(ns, spectrum, ocean_mask, depth_class, freq_speed, coupling, source, gain_table):
    vmem, hbm = pl.BlockSpec(memory_space=pltpu.VMEM), pl.BlockSpec(memory_space=pl.ANY)
    dma = pltpu.SemaphoreType.DMA
    out = pl.pallas_call(
        functools.partial(kernel, ns),
        out_shape=jax.ShapeDtypeStruct((LOCAL * 8, 128), F32),
        in_specs=[vmem, vmem, vmem, pl.BlockSpec(memory_space=pltpu.SMEM), hbm, hbm, vmem],
        out_specs=vmem,
        scratch_shapes=[
            pltpu.VMEM((2, BINS, BINS), BF16),
            pltpu.VMEM((12, BINS, 256), BF16),
            pltpu.VMEM((12, 1536, 256), BF16),
            pltpu.VMEM((2048, 512), BF16),
            pltpu.VMEM((NSPEC, 192, 176), BF16),
            pltpu.VMEM((12, 12, 24, 128), F32),
            pltpu.VMEM((12, 12, 24, 128), F32),
            pltpu.VMEM((12, 128, 128), F32),
            pltpu.VMEM((12, 128, 256), F32),
            pltpu.VMEM((128, 1536), BF16),
            pltpu.VMEM((128, 1536), BF16),
            pltpu.VMEM((12, 128, 128), F32),
            pltpu.VMEM((12, 8, 128), F32),
            pltpu.VMEM((16, 32, 128), F32),
            pltpu.VMEM((3, 16, 128), F32),
            pltpu.VMEM((8, ROWS, 128), F32),
            pltpu.VMEM((8, ROWS, 128), F32),
            pltpu.VMEM((8, ROWS, 128), F32),
            pltpu.VMEM((12, 4, 8, 128), F32),
            pltpu.VMEM((12, 8, 128), F32),
            pltpu.VMEM((PHASES, 12, 4, 16, 128), F32),
            pltpu.VMEM((PHASES, 12, 4, 8, 128), F32),
            pltpu.VMEM((PHASES, 12, 8, 128), F32),
            pltpu.VMEM((128, 128), F32),
            pltpu.VMEM((152, 128), F32),
            pltpu.VMEM((128, 128), F32),
            pltpu.VMEM((8, 128), F32),
            pltpu.VMEM((2, 8, 128), F32),
            dma((2,)), dma((8, 4)), dma((8, 4)), dma((8, 4)), dma((8, 4)), dma,
            dma((PHASES, 4, 3)), dma((PHASES, 4, 3)), dma((2,)), dma((2,)),
        ],
        compiler_params=pltpu.CompilerParams(
            collective_id=0, has_side_effects=True, vmem_limit_bytes=56 * 2**20),
        cost_estimate=pl.CostEstimate(flops=12 * 10**9, bytes_accessed=9 * 10**6, transcendentals=0),
        name="wave_steps",
    )(spectrum.reshape(LOCAL * 8, 128), ocean_mask, depth_class, freq_speed, coupling, source, gain_table)
    return out.reshape(LOCAL, 8, 128)


def solution(mesh):
    placed = (P("spec", "space", None), P("space", None), P("space", None), P(), P(), P(), P())
    return jax.shard_map(
        functools.partial(shards, mesh.shape["space"]), mesh=mesh, in_specs=placed,
        out_specs=P("spec", "space", None), check_vma=False)
```

```python
import functools
import math

import jax
import jax.numpy as jnp
from jax import lax
from jax.experimental import pallas as pl
from jax.experimental.pallas import tpu as pltpu
from jax.sharding import PartitionSpec as P

MESH = pl.DeviceIdType.MESH
F32, BF16, I32 = jnp.float32, jnp.bfloat16, jnp.int32
BINS, NDIR, NFREQ, CLASSES = 1296, 36, 36, 8
ITERS = 4
NSPEC, LOCAL = 8, 162
SLOT = 48
FULL = (5, 5, 4, 4)
BASE = (0, 48, 96, 136)
KEPT = (48, 48, 40, 40)
LIVE = (45, 45, 36, 36)
ROWS = 176
QUADS = (0, 2, 1, 3)
LOWX, LOWY = (True, False, False, True), (True, False, True, False)
PAIRS = ((0, 0), (1, 0), (1, 1), (2, 1), (3, 1), (3, 2), (4, 2), (5, 2))
PHASES = ITERS + 1


def off_j(q):
    return 4 if LOWY[q] else 0


def off_i(q):
    return 8 if LOWX[q] else 0


def block_of(r, half):
    low = lax.rem(r // 4 + half, 2)
    x = lax.rem(r, 4)
    return jnp.where(low == 0, x, 7 - x)


def owner_of(c, half):
    x = jnp.where(c < 4, c, 7 - c)
    return lax.rem(c // 4 + half, 2) * 4 + x


def swap_blocks(parts):
    lane = lax.broadcasted_iota(I32, parts[0].shape, 1)
    for h in (4, 2, 1):
        keep = (lane & (16 * h)) == 0
        new = list(parts)
        for j in range(8):
            if j & h == 0:
                a, b = parts[j], parts[j + h]
                new[j] = jnp.where(keep, a, pltpu.roll(b, 16 * h, 1))
                new[j + h] = jnp.where(keep, pltpu.roll(a, 128 - 16 * h, 1), b)
        parts = new
    return parts


def local_bin(rel, idx):
    many = rel < 2
    whole = jnp.where(many, 40, 32)
    runs = jnp.where(many, 5, 4)
    first = 36 * (idx >> 3) + (idx & 7)
    last = 36 * (idx - whole) + 8
    return jnp.where(idx < whole, first + 9 * rel, jnp.where(idx < whole + runs, last + 9 * rel, -10000))


def places(q, g, shape):
    slot = 128 * g + lax.broadcasted_iota(I32, shape, len(shape) - 1)
    r = jnp.zeros_like(slot)
    for k in range(1, 8):
        r = r + (slot >= SLOT * k).astype(I32)
    return r, q ^ (2 * (r & 1)), slot - SLOT * r


def relative(q, r):
    return QUADS[q] ^ (2 * (r & 1))


def kernel(ns, spectrum_ref, mask_ref, class_ref, speed_ref, coupling_ref, source_ref, gain_ref, result_ref,
           x_ref, out_ref, natural, turned, weights, pick, lift, e0, e1, slope, part, xb, yb, gains, gain_rows, mask, coef,
           send_a, land_a, land_b, ys, xs, cs, yl, xl, cl, tile, strip, kind, mask_own, mask_land,
           w_sem, a_send, a_recv, b_send, b_recv, own_sem, x_sem, o_sem, h_send, h_recv, m_send, m_recv):
    r = lax.axis_index("spec")
    s = lax.axis_index("space")
    half = s // (ns // 2)
    c = block_of(r, half)

    def at(dc, ds):
        cc, ss = jnp.clip(c + dc, 0, NSPEC - 1), jnp.clip(s + ds, 0, ns - 1)
        return (ss, owner_of(cc, ss // (ns // 2)))

    def there(dc, ds):
        ok = None
        for cond in ([c + dc >= 0, c + dc < NSPEC] if dc else []) + ([s + ds >= 0, s + ds < ns] if ds else []):
            ok = cond if ok is None else jnp.logical_and(ok, cond)
        return ok

    take_x = pltpu.make_async_copy(spectrum_ref, x_ref, x_sem)
    take_x.start()
    loads = [pltpu.make_async_copy(ref, natural.at[m], w_sem.at[m]) for m, ref in enumerate((coupling_ref, source_ref))]
    for slot in range(NSPEC):
        for rel in range(4):
            end = BASE[rel] + KEPT[rel]
            land_a[slot, end - 8:end, :] = jnp.zeros((8, 128), F32)
    barrier = pltpu.get_barrier_semaphore()
    around = [(dc, ds) for ds in (-1, 1) for dc in (-1, 0, 1)]
    for k in range(1, NSPEC):
        pl.semaphore_signal(barrier, inc=1, device_id=(s, lax.rem(r + k, NSPEC)), device_id_type=MESH)
    for dc, ds in around:
        @pl.when(there(dc, ds))
        def _():
            pl.semaphore_signal(barrier, inc=1, device_id=at(dc, ds), device_id_type=MESH)

    for copy in loads:
        copy.start()
    mask_own[...] = mask_ref[...].astype(F32)

    def clear(qg, _):
        e0[qg] = jnp.zeros((12, 24, 128), F32)
        e1[qg] = jnp.zeros((12, 24, 128), F32)
        return 0
    lax.fori_loop(0, 12, clear, 0)
    take_x.wait()

    for rel in range(4):
        for f in range(FULL[rel]):
            parts = [x_ref[pl.ds((36 * f + 9 * rel) * 8 + j, 8, stride=8), :] for j in range(8)]
            for cc, block in enumerate(swap_blocks(parts)):
                send_a[cc, BASE[rel] + 8 * f:BASE[rel] + 8 * f + 8, :] = block
        n = FULL[rel]
        parts = [x_ref[pl.ds((9 * rel + 8) * 8 + j, n, stride=288), :] for j in range(8)]
        for cc, block in enumerate(swap_blocks(parts)):
            send_a[cc, BASE[rel] + 8 * n:BASE[rel] + 8 * n + 8, :] = jnp.zeros((8, 128), F32)
            send_a[cc, BASE[rel] + 8 * n:BASE[rel] + 9 * n, :] = block

    beside = (c > 0).astype(I32) + (c < NSPEC - 1).astype(I32)
    beyond = (s > 0).astype(I32) + (s < ns - 1).astype(I32)
    pl.semaphore_wait(barrier, NSPEC - 1 + beyond * (1 + beside))

    def a_copy(k, rel, incoming=False):
        peer = lax.rem(r + k, NSPEC)
        slot = peer if incoming else r
        rows = pl.ds(BASE[rel], LIVE[rel])
        return pltpu.make_async_remote_copy(
            src_ref=send_a.at[block_of(peer, half), rows], dst_ref=land_a.at[slot, rows],
            send_sem=a_send.at[k, rel], recv_sem=a_recv.at[slot, rel], device_id=(s, peer), device_id_type=MESH)

    for rel in range(4):
        for k in range(1, NSPEC):
            a_copy(k, rel).start()
    own_a = pltpu.make_async_copy(send_a.at[c], land_a.at[r], own_sem)
    own_a.start()

    def mask_copy(ds, incoming=False):
        k = (1 if ds < 0 else 0) if not incoming else (0 if ds < 0 else 1)
        return pltpu.make_async_remote_copy(
            src_ref=mask_own, dst_ref=mask_land.at[k], send_sem=m_send.at[k], recv_sem=m_recv.at[k],
            device_id=at(0, ds), device_id_type=MESH)

    for ds in (-1, 1):
        @pl.when(there(0, ds))
        def _():
            mask_copy(ds).start()

    row = lax.broadcasted_iota(I32, (16, 128), 0)
    quad = (row >= 3).astype(I32) + (row >= 6).astype(I32) + (row >= 9).astype(I32)
    group = row - 3 * quad
    quad = jnp.where(quad == 1, 2, jnp.where(quad == 2, 1, quad))
    home, rel, idx = places(quad, group, (16, 128))
    here = local_bin(rel, idx)
    many = rel < 2
    whole = jnp.where(many, 40, 32)
    run = jnp.where(idx < whole, idx >> 3, idx - whole)
    step = jnp.where(idx < whole, idx & 7, 8)
    freq = ((9 * home) >> 1) + run + jnp.where(many, 0, home & 1)
    group_speed = jnp.zeros((16, 128), F32)
    for k in range(NFREQ):
        group_speed = jnp.where(freq == k, speed_ref[k], group_speed)
    group_speed = jnp.where(here >= 0, group_speed, 0.0)
    cosine, sine = jnp.zeros((16, 128), F32), jnp.zeros((16, 128), F32)
    for k in range(9):
        cosine = jnp.where(step == k, math.cos(2.0 * math.pi * (k + 0.5) / NDIR), cosine)
        sine = jnp.where(step == k, math.sin(2.0 * math.pi * (k + 0.5) / NDIR), sine)
    even = (quad & 1) == 0
    ax = group_speed * jnp.where(even, cosine, sine)
    ay = group_speed * jnp.where(even, sine, cosine)
    coef[0] = 1.0 - ax - ay
    coef[1] = ax
    coef[2] = ay

    for k, (t, g) in enumerate(PAIRS):
        rows = 16 if t == 5 else 256
        for q in range(4):
            home, rel, idx = places(jnp.full((1, 128), QUADS[q], I32), g, (1, 128))
            want = LOCAL * home + local_bin(rel, idx) - 256 * t
            hit = lax.broadcasted_iota(I32, (rows, 128), 0) == want
            pick[256 * k:256 * k + rows, 128 * q:128 * q + 128] = jnp.where(hit, 1.0, 0.0).astype(BF16)

    def to_quadrants(lhs, g):
        first, start, depth = ((0, 0, 512), (2, 256, 768), (5, 768, 528))[g]
        return jnp.dot(lhs(start, depth), pick[256 * first:256 * first + depth, :], preferred_element_type=F32)

    for rr in range(NSPEC):
        for q in range(4):
            spot = lax.broadcasted_iota(I32, (SLOT, 176), 0)
            want = local_bin(jnp.full((SLOT, 176), relative(q, rr), I32), spot) + 2 * rr
            hit = lax.broadcasted_iota(I32, (SLOT, 176), 1) == want
            lift[rr, SLOT * q:SLOT * q + SLOT, :] = jnp.where(hit, 1.0, 0.0).astype(BF16)

    table = gain_ref[...]
    high = table.astype(BF16).astype(F32)
    mid = (table - high).astype(BF16).astype(F32)
    low = table - high - mid
    thirds = jnp.concatenate([high, mid, low, jnp.zeros_like(low)], axis=0).astype(BF16)
    for g in range(3):
        total = to_quadrants(lambda at_, n: thirds[:, at_:at_ + n], g)
        for q in range(4):
            third = total[:, 128 * q:128 * q + 128]
            gain_rows[3 * q + g] = third[0:8] + third[8:16] + third[16:24]

    for copy in loads:
        copy.wait()
    for m in range(2):
        def columns(k, _, m=m):
            rows = pl.ds(pl.multiple_of(432 * k, 16), 432)
            for g in range(3):
                total = to_quadrants(lambda at_, n: natural[m, rows, at_:at_ + n], g).astype(BF16)
                for q in range(4):
                    turned[3 * q + g, rows, 128 * m:128 * m + 128] = total[:, 128 * q:128 * q + 128]
            return 0
        lax.fori_loop(0, 3, columns, 0)

    for k, ds in ((0, -1), (1, 1)):
        @pl.when(there(0, ds))
        def _():
            mask_copy(ds, incoming=True).wait_recv()
            mask_copy(ds).wait_send()
            tile[16 * k:16 * k + 8, :] = mask_land[k]

        @pl.when(jnp.logical_not(there(0, ds)))
        def _():
            tile[16 * k:16 * k + 8, :] = jnp.zeros((8, 128), F32)
    tile[8:16, :] = mask_own[...]
    tile[24:32, :] = class_ref[...].astype(F32)
    tile[32:128, :] = jnp.zeros((96, 128), F32)
    strip[0:8, :] = jnp.zeros((8, 128), F32)
    strip[136:152, :] = jnp.zeros((16, 128), F32)
    strip[8:136, :] = tile[...].T
    near = strip[pl.ds(pl.multiple_of(16 * c, 16), 32), :]
    for j in range(16):
        mask[j] = jnp.broadcast_to(near[:, j + 4:j + 5], (32, 128))
    for j in range(8):
        kind[16 * j:16 * j + 16, :] = jnp.broadcast_to(near[8:24, 24 + j:25 + j], (16, 128))

    def fill(qg, _):
        which = kind[...]
        value = jnp.zeros((128, 128), F32)
        for k in range(CLASSES):
            value = jnp.where(which == float(k), gain_rows[qg, k:k + 1, :], value)
        gains[qg] = value
        return 0
    lax.fori_loop(0, 12, fill, 0)

    def heading(q):
        return (1 if LOWX[q] else -1), (1 if LOWY[q] else -1)

    def edge(q, kind):
        dx, dy = heading(q)
        return ((0, dy), (dx, 0), (dx, dy))[kind]

    def edge_copy(p, q, kind):
        dc, ds = edge(q, kind)
        groups = pl.ds(3 * q, 3)
        src, dst = ((ys, yl), (xs, xl), (cs, cl))[kind]
        return pltpu.make_async_remote_copy(
            src_ref=src.at[groups], dst_ref=dst.at[p, groups], send_sem=h_send.at[p, q, kind],
            recv_sem=h_recv.at[p, q, kind], device_id=at(dc, ds), device_id_type=MESH)

    def corner(q, landed):
        for d, (n, at_) in enumerate(((3, 0), (2, 3), (1, 5))):
            j = (3 - d if landed else 11 - d) if LOWY[q] else (8 + d if landed else d)
            i = ((8 if landed else 24) - n) if LOWX[q] else (16 if landed else 0)
            yield n, at_, j, i

    def send_edges(p, q):
        i = 20 if LOWX[q] else 0
        jy = 8 if LOWY[q] else 0
        groups = range(3 * q, 3 * q + 3)

        def start(kind):
            @pl.when(there(*edge(q, kind)))
            def _():
                edge_copy(p, q, kind).start()

        for qg in groups:
            for n, at_, j, ii in corner(q, False):
                cs[qg, at_:at_ + n, :] = e0[qg, j, ii:ii + n, :]
        start(2)
        for qg in groups:
            ys[qg] = e0[qg, jy:jy + 4, off_i(q):off_i(q) + 16, :]
        start(0)
        for qg in groups:
            for j in range(8):
                xs[qg, j // 2, 4 * (j % 2):4 * (j % 2) + 4, :] = e0[qg, off_j(q) + j, i:i + 4, :]
        start(1)

    def take_edges(p, q):
        i = 4 if LOWX[q] else 16
        jh = 0 if LOWY[q] else 8
        groups = range(3 * q, 3 * q + 3)
        for kind in range(3):
            dc, ds = edge(q, kind)

            @pl.when(there(-dc, -ds))
            def _():
                edge_copy(p, q, kind).wait_recv()
                for qg in groups:
                    if kind == 0:
                        e0[qg, jh:jh + 4, off_i(q):off_i(q) + 16, :] = yl[p, qg]
                    elif kind == 1:
                        for j in range(8):
                            e0[qg, off_j(q) + j, i:i + 4, :] = xl[p, qg, j // 2, 4 * (j % 2):4 * (j % 2) + 4, :]
                    else:
                        for n, at_, j, ii in corner(q, True):
                            e0[qg, j, ii:ii + n, :] = cl[p, qg, at_:at_ + n, :]

    def settle_edges(p):
        for q in range(4):
            for kind in range(3):
                @pl.when(there(*edge(q, kind)))
                def _():
                    edge_copy(p, q, kind).wait_send()

    def substep(q, t):
        src, dst = (e0, e1) if t % 2 == 0 else (e1, e0)
        if LOWY[q]:
            j0, n, jm = t + 1, 11 - t, 0
        else:
            j0, n, jm = 0, 11 - t, 4
        if LOWX[q]:
            di, im, starts = -1, 0, (8, 16) + (() if t == 3 else (1,))
        else:
            di, im, starts = 1, 8, (0, 8) + (() if t == 3 else (15,))

        groups = slice(3 * q, 3 * q + 3)
        c0, cx, cy = (coef[k, groups, :].reshape(3, 1, 1, 128) for k in range(3))
        for i in starts:
            for first in range(j0, j0 + n, 4):
                m = min(4, j0 + n - first)
                if LOWY[q]:
                    both = src[groups, first - 1:first + m, i:i + 8, :]
                    mid, across = both[:, 1:], both[:, :-1]
                else:
                    both = src[groups, first:first + m + 1, i:i + 8, :]
                    mid, across = both[:, :-1], both[:, 1:]
                along = src[groups, first:first + m, i + di:i + di + 8, :]
                sea = mask[first + jm:first + jm + m, i + im:i + im + 8, :][None]
                dst[groups, first:first + m, i:i + 8, :] = (c0 * mid + cx * along + cy * across) * sea

    def interior(q):
        return slice(off_j(q), off_j(q) + 8), slice(off_i(q), off_i(q) + 16)

    def narrow(q):
        js, is_ = interior(q)
        for g in range(3):
            qg = 3 * q + g
            xb[:, 128 * qg:128 * qg + 128] = e0[qg, js, is_, :].reshape(128, 128).astype(BF16)

    def first_half(qg):
        part[qg] = jnp.dot(xb[:, :768], weights[qg, :768, :], preferred_element_type=F32)

    def second_half(qg):
        got = part[qg] + jnp.dot(xb[:, 768:], weights[qg, 768:, :], preferred_element_type=F32)
        change = gains[qg] * got[:, :128] + got[:, 128:]
        slope[qg] = change
        js, is_ = interior(qg // 3)
        state = e0[qg, js, is_, :].reshape(128, 128)
        yb[:, 128 * qg:128 * qg + 128] = (state + change).astype(BF16)

    def finish(q):
        js, is_ = interior(q)

        for qg in range(3 * q, 3 * q + 3):
            got = jnp.dot(yb[...], weights[qg], preferred_element_type=F32)
            change = gains[qg] * got[:, :128] + got[:, 128:]
            state = e0[qg, js, is_, :].reshape(128, 128)
            e0[qg, js, is_, :] = (state + 0.5 * (slope[qg] + change)).reshape(8, 16, 128)

    own_a.wait()
    for rel in range(4):
        for k in range(1, NSPEC):
            a_copy(k, rel, incoming=True).wait_recv()
    for q in range(4):
        for g in range(3):
            pieces = []
            for rr in range(NSPEC):
                a, b = max(SLOT * rr, 128 * g) - SLOT * rr, min(SLOT * rr + SLOT, 128 * g + 128) - SLOT * rr
                if a >= b:
                    continue
                rel = relative(q, rr)
                cut = min(b, KEPT[rel])
                if a < cut:
                    pieces.append(land_a[rr, BASE[rel] + a:BASE[rel] + cut, :])
                if cut < b:
                    pieces.append(jnp.zeros((b - max(a, cut), 128), F32))
            e0[3 * q + g, off_j(q):off_j(q) + 8, off_i(q):off_i(q) + 16, :] = (
                jnp.concatenate(pieces, axis=0).T.reshape(8, 16, 128))
        send_edges(0, q)

    def lines(qg, _):
        for rr in range(NSPEC):
            got = jnp.dot(lift[rr], turned[qg, 160 * rr:160 * rr + 176, :], preferred_element_type=F32).astype(BF16)
            for q in range(4):
                weights[qg, 384 * q + SLOT * rr:384 * q + SLOT * rr + SLOT, :] = got[SLOT * q:SLOT * q + SLOT]
        return 0
    lax.fori_loop(0, 12, lines, 0)

    def phase(p, _):
        for q in range(4):
            take_edges(p, q)

            @pl.when(p > 0)
            def _():
                substep(q, 0)
                substep(q, 1)
            substep(q, 2)
            substep(q, 3)
            narrow(q)
            if q == 1:
                for qg in range(12):
                    first_half(qg)
        for qg in range(12):
            second_half(qg)
        settle_edges(p)
        for q in range(4):
            finish(q)
            send_edges(p + 1, q)
        return 0

    lax.fori_loop(0, ITERS, phase, 0)

    for rel in range(4):
        for k in range(1, NSPEC):
            a_copy(k, rel).wait_send()

    def b_copy(k, q, odd, incoming=False):
        peer = lax.rem(r + k, NSPEC)
        slot = block_of(peer, half) if incoming else c
        rel = relative(q, odd)
        rows = pl.ds(BASE[rel], LIVE[rel])
        return pltpu.make_async_remote_copy(
            src_ref=send_a.at[peer, rows], dst_ref=land_b.at[slot, rows],
            send_sem=b_send.at[k, q], recv_sem=b_recv.at[slot, rel], device_id=(s, peer), device_id_type=MESH)

    for q in range(4):
        take_edges(ITERS, q)
        substep(q, 2)
        substep(q, 3)
        js, is_ = interior(q)
        for g in range(3):
            block = e0[3 * q + g, js, is_, :].reshape(128, 128).T
            for rr in range(NSPEC):
                a, b = max(SLOT * rr, 128 * g), min(SLOT * rr + SLOT, 128 * g + 128)
                rel = relative(q, rr)
                b = min(b, SLOT * rr + KEPT[rel])
                if a < b:
                    send_a[rr, BASE[rel] + a - SLOT * rr:BASE[rel] + b - SLOT * rr, :] = block[a - 128 * g:b - 128 * g]
        for k in range(1, NSPEC):
            for odd in range(2):
                @pl.when(lax.rem(r + k, 2) == odd)
                def _():
                    b_copy(k, q, odd).start()
    settle_edges(ITERS)
    own_b = pltpu.make_async_copy(send_a.at[r], land_b.at[c], own_sem)
    own_b.start()

    def put(rel):
        n = FULL[rel]
        for f in range(n):
            rows = slice(BASE[rel] + 8 * f, BASE[rel] + 8 * f + 8)
            parts = swap_blocks([land_b[cc, rows, :] for cc in range(8)])
            for j in range(8):
                out_ref[pl.ds((36 * f + 9 * rel) * 8 + j, 8, stride=8), :] = parts[j]
        parts = swap_blocks([land_b[cc, BASE[rel] + 8 * n:BASE[rel] + 9 * n, :] for cc in range(8)])
        for j in range(8):
            out_ref[pl.ds((9 * rel + 8) * 8 + j, n, stride=288), :] = parts[j]
        for f in range(n):
            out_copy(rel, f).start()

    def out_copy(rel, f):
        rows = pl.ds((36 * f + 9 * rel) * 8, 72)
        return pltpu.make_async_copy(out_ref.at[rows], result_ref.at[rows], o_sem.at[rel, f])

    own_b.wait()
    for odd in range(2):
        @pl.when(lax.rem(r, 2) == odd)
        def _():
            for q in range(4):
                for k in range(1, NSPEC):
                    b_copy(k, q, odd, incoming=True).wait_recv()
                put(relative(q, odd))
    for k in range(1, NSPEC):
        for q in range(4):
            for odd in range(2):
                @pl.when(lax.rem(r + k, 2) == odd)
                def _():
                    b_copy(k, q, odd).wait_send()
    for rel in range(4):
        for f in range(FULL[rel]):
            out_copy(rel, f).wait()


def shards(ns, spectrum, ocean_mask, depth_class, freq_speed, coupling, source, gain_table):
    vmem, hbm = pl.BlockSpec(memory_space=pltpu.VMEM), pl.BlockSpec(memory_space=pl.ANY)
    dma = pltpu.SemaphoreType.DMA
    out = pl.pallas_call(
        functools.partial(kernel, ns),
        out_shape=jax.ShapeDtypeStruct((LOCAL * 8, 128), F32),
        in_specs=[hbm, vmem, vmem, pl.BlockSpec(memory_space=pltpu.SMEM), hbm, hbm, vmem],
        out_specs=hbm,
        scratch_shapes=[
            pltpu.VMEM((LOCAL * 8, 128), F32),
            pltpu.VMEM((LOCAL * 8, 128), F32),
            pltpu.VMEM((2, BINS, BINS), BF16),
            pltpu.VMEM((12, BINS, 256), BF16),
            pltpu.VMEM((12, 1536, 256), BF16),
            pltpu.VMEM((2048, 512), BF16),
            pltpu.VMEM((NSPEC, 192, 176), BF16),
            pltpu.VMEM((12, 12, 24, 128), F32),
            pltpu.VMEM((12, 12, 24, 128), F32),
            pltpu.VMEM((12, 128, 128), F32),
            pltpu.VMEM((12, 128, 256), F32),
            pltpu.VMEM((128, 1536), BF16),
            pltpu.VMEM((128, 1536), BF16),
            pltpu.VMEM((12, 128, 128), F32),
            pltpu.VMEM((12, 8, 128), F32),
            pltpu.VMEM((16, 32, 128), F32),
            pltpu.VMEM((3, 16, 128), F32),
            pltpu.VMEM((8, ROWS, 128), F32),
            pltpu.VMEM((8, ROWS, 128), F32),
            pltpu.VMEM((8, ROWS, 128), F32),
            pltpu.VMEM((12, 4, 16, 128), F32),
            pltpu.VMEM((12, 4, 8, 128), F32),
            pltpu.VMEM((12, 8, 128), F32),
            pltpu.VMEM((PHASES, 12, 4, 16, 128), F32),
            pltpu.VMEM((PHASES, 12, 4, 8, 128), F32),
            pltpu.VMEM((PHASES, 12, 8, 128), F32),
            pltpu.VMEM((128, 128), F32),
            pltpu.VMEM((152, 128), F32),
            pltpu.VMEM((128, 128), F32),
            pltpu.VMEM((8, 128), F32),
            pltpu.VMEM((2, 8, 128), F32),
            dma((2,)), dma((8, 4)), dma((8, 4)), dma((8, 4)), dma((8, 4)), dma, dma, dma((4, 5)),
            dma((PHASES, 4, 3)), dma((PHASES, 4, 3)), dma((2,)), dma((2,)),
        ],
        compiler_params=pltpu.CompilerParams(
            collective_id=0, has_side_effects=True, vmem_limit_bytes=56 * 2**20),
        cost_estimate=pl.CostEstimate(flops=12 * 10**9, bytes_accessed=9 * 10**6, transcendentals=0),
        name="wave_steps",
    )(spectrum.reshape(LOCAL * 8, 128), ocean_mask, depth_class, freq_speed, coupling, source, gain_table)
    return out.reshape(LOCAL, 8, 128)


def solution(mesh):
    placed = (P("spec", "space", None), P("space", None), P("space", None), P(), P(), P(), P())
    return jax.shard_map(
        functools.partial(shards, mesh.shape["space"]), mesh=mesh, in_specs=placed,
        out_specs=P("spec", "space", None), check_vma=False)
```

```python
import functools
import math

import jax
import jax.numpy as jnp
from jax import lax
from jax.experimental import pallas as pl
from jax.experimental.pallas import tpu as pltpu
from jax.sharding import PartitionSpec as P

MESH = pl.DeviceIdType.MESH
F32, BF16, I32 = jnp.float32, jnp.bfloat16, jnp.int32
BINS, NDIR, NFREQ, CLASSES = 1296, 36, 36, 8
ITERS = 4
NSPEC, LOCAL = 8, 162
SLOT = 48
FULL = (5, 5, 4, 4)
BASE = (0, 48, 96, 136)
KEPT = (48, 48, 40, 40)
LIVE = (45, 45, 36, 36)
ROWS = 176
QUADS = (0, 2, 1, 3)
LOWX, LOWY = (True, False, False, True), (True, False, True, False)
PAIRS = ((0, 0), (1, 0), (1, 1), (2, 1), (3, 1), (3, 2), (4, 2), (5, 2))
PHASES = ITERS + 1


def off_j(q):
    return 4 if LOWY[q] else 0


def off_i(q):
    return 8 if LOWX[q] else 0


def block_of(r, half):
    low = lax.rem(r // 4 + half, 2)
    x = lax.rem(r, 4)
    return jnp.where(low == 0, x, 7 - x)


def owner_of(c, half):
    x = jnp.where(c < 4, c, 7 - c)
    return lax.rem(c // 4 + half, 2) * 4 + x


def swap_blocks(parts):
    lane = lax.broadcasted_iota(I32, parts[0].shape, 1)
    for h in (4, 2, 1):
        keep = (lane & (16 * h)) == 0
        new = list(parts)
        for j in range(8):
            if j & h == 0:
                a, b = parts[j], parts[j + h]
                new[j] = jnp.where(keep, a, pltpu.roll(b, 16 * h, 1))
                new[j + h] = jnp.where(keep, pltpu.roll(a, 128 - 16 * h, 1), b)
        parts = new
    return parts


def local_bin(rel, idx):
    many = rel < 2
    whole = jnp.where(many, 40, 32)
    runs = jnp.where(many, 5, 4)
    first = 36 * (idx >> 3) + (idx & 7)
    last = 36 * (idx - whole) + 8
    return jnp.where(idx < whole, first + 9 * rel, jnp.where(idx < whole + runs, last + 9 * rel, -10000))


def places(q, g, shape):
    slot = 128 * g + lax.broadcasted_iota(I32, shape, len(shape) - 1)
    r = jnp.zeros_like(slot)
    for k in range(1, 8):
        r = r + (slot >= SLOT * k).astype(I32)
    return r, q ^ (2 * (r & 1)), slot - SLOT * r


def relative(q, r):
    return QUADS[q] ^ (2 * (r & 1))


def kernel(ns, spectrum_ref, mask_ref, class_ref, speed_ref, coupling_ref, source_ref, gain_ref, result_ref,
           x_ref, out_ref, natural, turned, weights, pick, lift, e0, e1, slope, part, xb, yb, gains, gain_rows, mask, coef,
           send_a, land_a, land_b, ys, xs, cs, yl, xl, cl, tile, strip, kind, mask_own, mask_land,
           w_sem, a_send, a_recv, b_send, b_recv, own_sem, x_sem, o_sem, h_send, h_recv, m_send, m_recv):
    r = lax.axis_index("spec")
    s = lax.axis_index("space")
    half = s // (ns // 2)
    c = block_of(r, half)

    def at(dc, ds):
        cc, ss = jnp.clip(c + dc, 0, NSPEC - 1), jnp.clip(s + ds, 0, ns - 1)
        return (ss, owner_of(cc, ss // (ns // 2)))

    def there(dc, ds):
        ok = None
        for cond in ([c + dc >= 0, c + dc < NSPEC] if dc else []) + ([s + ds >= 0, s + ds < ns] if ds else []):
            ok = cond if ok is None else jnp.logical_and(ok, cond)
        return ok

    take_x = pltpu.make_async_copy(spectrum_ref, x_ref, x_sem)
    take_x.start()
    loads = [pltpu.make_async_copy(ref, natural.at[m], w_sem.at[m]) for m, ref in enumerate((coupling_ref, source_ref))]
    for slot in range(NSPEC):
        for rel in range(4):
            end = BASE[rel] + KEPT[rel]
            land_a[slot, end - 8:end, :] = jnp.zeros((8, 128), F32)
    barrier = pltpu.get_barrier_semaphore()
    around = [(dc, ds) for ds in (-1, 1) for dc in (-1, 0, 1)]
    for k in range(1, NSPEC):
        pl.semaphore_signal(barrier, inc=1, device_id=(s, lax.rem(r + k, NSPEC)), device_id_type=MESH)
    for dc, ds in around:
        @pl.when(there(dc, ds))
        def _():
            pl.semaphore_signal(barrier, inc=1, device_id=at(dc, ds), device_id_type=MESH)

    for copy in loads:
        copy.start()
    mask_own[...] = mask_ref[...].astype(F32)

    def clear(qg, _):
        e0[qg] = jnp.zeros((12, 24, 128), F32)
        e1[qg] = jnp.zeros((12, 24, 128), F32)
        return 0
    lax.fori_loop(0, 12, clear, 0)
    take_x.wait()

    for rel in range(4):
        for f in range(FULL[rel]):
            parts = [x_ref[pl.ds((36 * f + 9 * rel) * 8 + j, 8, stride=8), :] for j in range(8)]
            for cc, block in enumerate(swap_blocks(parts)):
                send_a[cc, BASE[rel] + 8 * f:BASE[rel] + 8 * f + 8, :] = block
        n = FULL[rel]
        parts = [x_ref[pl.ds((9 * rel + 8) * 8 + j, n, stride=288), :] for j in range(8)]
        for cc, block in enumerate(swap_blocks(parts)):
            send_a[cc, BASE[rel] + 8 * n:BASE[rel] + 8 * n + 8, :] = jnp.zeros((8, 128), F32)
            send_a[cc, BASE[rel] + 8 * n:BASE[rel] + 9 * n, :] = block

    beside = (c > 0).astype(I32) + (c < NSPEC - 1).astype(I32)
    beyond = (s > 0).astype(I32) + (s < ns - 1).astype(I32)
    pl.semaphore_wait(barrier, NSPEC - 1 + beyond * (1 + beside))

    def a_copy(k, rel, incoming=False):
        peer = lax.rem(r + k, NSPEC)
        slot = peer if incoming else r
        rows = pl.ds(BASE[rel], LIVE[rel])
        return pltpu.make_async_remote_copy(
            src_ref=send_a.at[block_of(peer, half), rows], dst_ref=land_a.at[slot, rows],
            send_sem=a_send.at[k, rel], recv_sem=a_recv.at[slot, rel], device_id=(s, peer), device_id_type=MESH)

    for rel in QUADS:
        for k in range(1, NSPEC):
            a_copy(k, rel).start()
    own_a = pltpu.make_async_copy(send_a.at[c], land_a.at[r], own_sem)
    own_a.start()

    def mask_copy(ds, incoming=False):
        k = (1 if ds < 0 else 0) if not incoming else (0 if ds < 0 else 1)
        return pltpu.make_async_remote_copy(
            src_ref=mask_own, dst_ref=mask_land.at[k], send_sem=m_send.at[k], recv_sem=m_recv.at[k],
            device_id=at(0, ds), device_id_type=MESH)

    for ds in (-1, 1):
        @pl.when(there(0, ds))
        def _():
            mask_copy(ds).start()

    row = lax.broadcasted_iota(I32, (16, 128), 0)
    quad = (row >= 3).astype(I32) + (row >= 6).astype(I32) + (row >= 9).astype(I32)
    group = row - 3 * quad
    quad = jnp.where(quad == 1, 2, jnp.where(quad == 2, 1, quad))
    home, rel, idx = places(quad, group, (16, 128))
    here = local_bin(rel, idx)
    many = rel < 2
    whole = jnp.where(many, 40, 32)
    run = jnp.where(idx < whole, idx >> 3, idx - whole)
    step = jnp.where(idx < whole, idx & 7, 8)
    freq = ((9 * home) >> 1) + run + jnp.where(many, 0, home & 1)
    group_speed = jnp.zeros((16, 128), F32)
    for k in range(NFREQ):
        group_speed = jnp.where(freq == k, speed_ref[k], group_speed)
    group_speed = jnp.where(here >= 0, group_speed, 0.0)
    cosine, sine = jnp.zeros((16, 128), F32), jnp.zeros((16, 128), F32)
    for k in range(9):
        cosine = jnp.where(step == k, math.cos(2.0 * math.pi * (k + 0.5) / NDIR), cosine)
        sine = jnp.where(step == k, math.sin(2.0 * math.pi * (k + 0.5) / NDIR), sine)
    even = (quad & 1) == 0
    ax = group_speed * jnp.where(even, cosine, sine)
    ay = group_speed * jnp.where(even, sine, cosine)
    coef[0] = 1.0 - ax - ay
    coef[1] = ax
    coef[2] = ay

    for k, (t, g) in enumerate(PAIRS):
        rows = 16 if t == 5 else 256
        for q in range(4):
            home, rel, idx = places(jnp.full((1, 128), QUADS[q], I32), g, (1, 128))
            want = LOCAL * home + local_bin(rel, idx) - 256 * t
            hit = lax.broadcasted_iota(I32, (rows, 128), 0) == want
            pick[256 * k:256 * k + rows, 128 * q:128 * q + 128] = jnp.where(hit, 1.0, 0.0).astype(BF16)

    def to_quadrants(lhs, g):
        first, start, depth = ((0, 0, 512), (2, 256, 768), (5, 768, 528))[g]
        return jnp.dot(lhs(start, depth), pick[256 * first:256 * first + depth, :], preferred_element_type=F32)

    for rr in range(NSPEC):
        for q in range(4):
            spot = lax.broadcasted_iota(I32, (SLOT, 176), 0)
            want = local_bin(jnp.full((SLOT, 176), relative(q, rr), I32), spot) + 2 * rr
            hit = lax.broadcasted_iota(I32, (SLOT, 176), 1) == want
            lift[rr, SLOT * q:SLOT * q + SLOT, :] = jnp.where(hit, 1.0, 0.0).astype(BF16)

    table = gain_ref[...]
    high = table.astype(BF16).astype(F32)
    mid = (table - high).astype(BF16).astype(F32)
    low = table - high - mid
    thirds = jnp.concatenate([high, mid, low, jnp.zeros_like(low)], axis=0).astype(BF16)
    for g in range(3):
        total = to_quadrants(lambda at_, n: thirds[:, at_:at_ + n], g)
        for q in range(4):
            third = total[:, 128 * q:128 * q + 128]
            gain_rows[3 * q + g] = third[0:8] + third[8:16] + third[16:24]

    for copy in loads:
        copy.wait()
    def columns(k, _):
        m = k // 3
        rows = pl.ds(pl.multiple_of(432 * lax.rem(k, 3), 16), 432)
        lanes = pl.ds(pl.multiple_of(128 * m, 128), 128)
        for g in range(3):
            total = to_quadrants(lambda at_, n: natural[m, rows, at_:at_ + n], g).astype(BF16)
            for q in range(4):
                turned[3 * q + g, rows, lanes] = total[:, 128 * q:128 * q + 128]
        return 0
    lax.fori_loop(0, 6, columns, 0)

    for k, ds in ((0, -1), (1, 1)):
        @pl.when(there(0, ds))
        def _():
            mask_copy(ds, incoming=True).wait_recv()
            mask_copy(ds).wait_send()
            tile[16 * k:16 * k + 8, :] = mask_land[k]

        @pl.when(jnp.logical_not(there(0, ds)))
        def _():
            tile[16 * k:16 * k + 8, :] = jnp.zeros((8, 128), F32)
    tile[8:16, :] = mask_own[...]
    tile[24:32, :] = class_ref[...].astype(F32)
    tile[32:128, :] = jnp.zeros((96, 128), F32)
    strip[0:8, :] = jnp.zeros((8, 128), F32)
    strip[136:152, :] = jnp.zeros((16, 128), F32)
    strip[8:136, :] = tile[...].T
    near = strip[pl.ds(pl.multiple_of(16 * c, 16), 32), :]
    for j in range(16):
        mask[j] = jnp.broadcast_to(near[:, j + 4:j + 5], (32, 128))
    for j in range(8):
        kind[16 * j:16 * j + 16, :] = jnp.broadcast_to(near[8:24, 24 + j:25 + j], (16, 128))

    def fill(qg, _):
        which = kind[...]
        value = jnp.zeros((128, 128), F32)
        for k in range(CLASSES):
            value = jnp.where(which == float(k), gain_rows[qg, k:k + 1, :], value)
        gains[qg] = value
        return 0
    lax.fori_loop(0, 12, fill, 0)

    def heading(q):
        return (1 if LOWX[q] else -1), (1 if LOWY[q] else -1)

    def edge(q, kind):
        dx, dy = heading(q)
        return ((0, dy), (dx, 0), (dx, dy))[kind]

    def edge_copy(p, q, kind):
        dc, ds = edge(q, kind)
        groups = pl.ds(3 * q, 3)
        src, dst = ((ys, yl), (xs, xl), (cs, cl))[kind]
        return pltpu.make_async_remote_copy(
            src_ref=src.at[groups], dst_ref=dst.at[p, groups], send_sem=h_send.at[p, q, kind],
            recv_sem=h_recv.at[p, q, kind], device_id=at(dc, ds), device_id_type=MESH)

    def corner(q, landed):
        for d, (n, at_) in enumerate(((3, 0), (2, 3), (1, 5))):
            j = (3 - d if landed else 11 - d) if LOWY[q] else (8 + d if landed else d)
            i = ((8 if landed else 24) - n) if LOWX[q] else (16 if landed else 0)
            yield n, at_, j, i

    def send_edges(p, q):
        i = 20 if LOWX[q] else 0
        jy = 8 if LOWY[q] else 0
        groups = range(3 * q, 3 * q + 3)

        def start(kind):
            @pl.when(there(*edge(q, kind)))
            def _():
                edge_copy(p, q, kind).start()

        for qg in groups:
            for n, at_, j, ii in corner(q, False):
                cs[qg, at_:at_ + n, :] = e0[qg, j, ii:ii + n, :]
        start(2)
        for qg in groups:
            ys[qg] = e0[qg, jy:jy + 4, off_i(q):off_i(q) + 16, :]
        start(0)
        for qg in groups:
            for j in range(8):
                xs[qg, j // 2, 4 * (j % 2):4 * (j % 2) + 4, :] = e0[qg, off_j(q) + j, i:i + 4, :]
        start(1)

    def take_edges(p, q):
        i = 4 if LOWX[q] else 16
        jh = 0 if LOWY[q] else 8
        groups = range(3 * q, 3 * q + 3)
        for kind in range(3):
            dc, ds = edge(q, kind)

            @pl.when(there(-dc, -ds))
            def _():
                edge_copy(p, q, kind).wait_recv()
                for qg in groups:
                    if kind == 0:
                        e0[qg, jh:jh + 4, off_i(q):off_i(q) + 16, :] = yl[p, qg]
                    elif kind == 1:
                        for j in range(8):
                            e0[qg, off_j(q) + j, i:i + 4, :] = xl[p, qg, j // 2, 4 * (j % 2):4 * (j % 2) + 4, :]
                    else:
                        for n, at_, j, ii in corner(q, True):
                            e0[qg, j, ii:ii + n, :] = cl[p, qg, at_:at_ + n, :]

    def settle_edges(p):
        for q in range(4):
            for kind in range(3):
                @pl.when(there(*edge(q, kind)))
                def _():
                    edge_copy(p, q, kind).wait_send()

    def substep(q, t):
        src, dst = (e0, e1) if t % 2 == 0 else (e1, e0)
        if LOWY[q]:
            j0, n, jm = t + 1, 11 - t, 0
        else:
            j0, n, jm = 0, 11 - t, 4
        if LOWX[q]:
            di, im, starts = -1, 0, (8, 16) + (() if t == 3 else (1,))
        else:
            di, im, starts = 1, 8, (0, 8) + (() if t == 3 else (15,))

        groups = slice(3 * q, 3 * q + 3)
        c0, cx, cy = (coef[k, groups, :].reshape(3, 1, 1, 128) for k in range(3))
        for i in starts:
            for first in range(j0, j0 + n, 4):
                m = min(4, j0 + n - first)
                if LOWY[q]:
                    both = src[groups, first - 1:first + m, i:i + 8, :]
                    mid, across = both[:, 1:], both[:, :-1]
                else:
                    both = src[groups, first:first + m + 1, i:i + 8, :]
                    mid, across = both[:, :-1], both[:, 1:]
                along = src[groups, first:first + m, i + di:i + di + 8, :]
                sea = mask[first + jm:first + jm + m, i + im:i + im + 8, :][None]
                dst[groups, first:first + m, i:i + 8, :] = (c0 * mid + cx * along + cy * across) * sea

    def interior(q):
        return slice(off_j(q), off_j(q) + 8), slice(off_i(q), off_i(q) + 16)

    def narrow(q):
        js, is_ = interior(q)
        for g in range(3):
            qg = 3 * q + g
            xb[:, 128 * qg:128 * qg + 128] = e0[qg, js, is_, :].reshape(128, 128).astype(BF16)

    def first_half(qg):
        part[qg] = jnp.dot(xb[:, :768], weights[qg, :768, :], preferred_element_type=F32)

    def second_half(qg):
        got = part[qg] + jnp.dot(xb[:, 768:], weights[qg, 768:, :], preferred_element_type=F32)
        change = gains[qg] * got[:, :128] + got[:, 128:]
        js, is_ = interior(qg // 3)
        state = e0[qg, js, is_, :].reshape(128, 128)
        slope[qg] = state + 0.5 * change
        yb[:, 128 * qg:128 * qg + 128] = (state + change).astype(BF16)

    def finish(q):
        js, is_ = interior(q)

        for qg in range(3 * q, 3 * q + 3):
            got = jnp.dot(yb[...], weights[qg], preferred_element_type=F32)
            change = gains[qg] * got[:, :128] + got[:, 128:]
            e0[qg, js, is_, :] = (slope[qg] + 0.5 * change).reshape(8, 16, 128)

    own_a.wait()
    for q in range(4):
        for rel in ((0, 2), (), (1, 3), ())[q]:
            for k in range(1, NSPEC):
                a_copy(k, rel, incoming=True).wait_recv()
        for g in range(3):
            pieces = []
            for rr in range(NSPEC):
                a, b = max(SLOT * rr, 128 * g) - SLOT * rr, min(SLOT * rr + SLOT, 128 * g + 128) - SLOT * rr
                if a >= b:
                    continue
                rel = relative(q, rr)
                cut = min(b, KEPT[rel])
                if a < cut:
                    pieces.append(land_a[rr, BASE[rel] + a:BASE[rel] + cut, :])
                if cut < b:
                    pieces.append(jnp.zeros((b - max(a, cut), 128), F32))
            e0[3 * q + g, off_j(q):off_j(q) + 8, off_i(q):off_i(q) + 16, :] = (
                jnp.concatenate(pieces, axis=0).T.reshape(8, 16, 128))
        send_edges(0, q)

    def lines(qg, _):
        for rr in range(NSPEC):
            got = jnp.dot(lift[rr], turned[qg, 160 * rr:160 * rr + 176, :], preferred_element_type=F32).astype(BF16)
            for q in range(4):
                weights[qg, 384 * q + SLOT * rr:384 * q + SLOT * rr + SLOT, :] = got[SLOT * q:SLOT * q + SLOT]
        return 0
    lax.fori_loop(0, 12, lines, 0)

    def phase(p, _):
        for q in range(4):
            take_edges(p, q)

            @pl.when(p > 0)
            def _():
                substep(q, 0)
                substep(q, 1)
            substep(q, 2)
            substep(q, 3)
            narrow(q)
            if q == 1:
                for qg in range(12):
                    first_half(qg)
        for qg in range(12):
            second_half(qg)
        settle_edges(p)
        for q in range(4):
            finish(q)
            send_edges(p + 1, q)
        return 0

    lax.fori_loop(0, ITERS, phase, 0)

    for rel in range(4):
        for k in range(1, NSPEC):
            a_copy(k, rel).wait_send()

    def b_copy(k, q, odd, incoming=False):
        peer = lax.rem(r + k, NSPEC)
        slot = block_of(peer, half) if incoming else c
        rel = relative(q, odd)
        rows = pl.ds(BASE[rel], LIVE[rel])
        return pltpu.make_async_remote_copy(
            src_ref=send_a.at[peer, rows], dst_ref=land_b.at[slot, rows],
            send_sem=b_send.at[k, q], recv_sem=b_recv.at[slot, rel], device_id=(s, peer), device_id_type=MESH)

    for q in range(4):
        take_edges(ITERS, q)
        substep(q, 2)
        substep(q, 3)
        js, is_ = interior(q)
        for g in range(3):
            block = e0[3 * q + g, js, is_, :].reshape(128, 128).T
            for rr in range(NSPEC):
                a, b = max(SLOT * rr, 128 * g), min(SLOT * rr + SLOT, 128 * g + 128)
                rel = relative(q, rr)
                b = min(b, SLOT * rr + KEPT[rel])
                if a < b:
                    send_a[rr, BASE[rel] + a - SLOT * rr:BASE[rel] + b - SLOT * rr, :] = block[a - 128 * g:b - 128 * g]
        for k in range(1, NSPEC):
            for odd in range(2):
                @pl.when(lax.rem(r + k, 2) == odd)
                def _():
                    b_copy(k, q, odd).start()
    settle_edges(ITERS)
    own_b = pltpu.make_async_copy(send_a.at[r], land_b.at[c], own_sem)
    own_b.start()

    def put(rel):
        n = FULL[rel]
        for f in range(n):
            rows = slice(BASE[rel] + 8 * f, BASE[rel] + 8 * f + 8)
            parts = swap_blocks([land_b[cc, rows, :] for cc in range(8)])
            for j in range(8):
                out_ref[pl.ds((36 * f + 9 * rel) * 8 + j, 8, stride=8), :] = parts[j]
        parts = swap_blocks([land_b[cc, BASE[rel] + 8 * n:BASE[rel] + 9 * n, :] for cc in range(8)])
        for j in range(8):
            out_ref[pl.ds((9 * rel + 8) * 8 + j, n, stride=288), :] = parts[j]
        for f in range(n):
            out_copy(rel, f).start()

    def out_copy(rel, f):
        rows = pl.ds((36 * f + 9 * rel) * 8, 72)
        return pltpu.make_async_copy(out_ref.at[rows], result_ref.at[rows], o_sem.at[rel, f])

    own_b.wait()
    for odd in range(2):
        @pl.when(lax.rem(r, 2) == odd)
        def _():
            for q in range(4):
                for k in range(1, NSPEC):
                    b_copy(k, q, odd, incoming=True).wait_recv()
                put(relative(q, odd))
    for k in range(1, NSPEC):
        for q in range(4):
            for odd in range(2):
                @pl.when(lax.rem(r + k, 2) == odd)
                def _():
                    b_copy(k, q, odd).wait_send()
    for rel in range(4):
        for f in range(FULL[rel]):
            out_copy(rel, f).wait()


def shards(ns, spectrum, ocean_mask, depth_class, freq_speed, coupling, source, gain_table):
    vmem, hbm = pl.BlockSpec(memory_space=pltpu.VMEM), pl.BlockSpec(memory_space=pl.ANY)
    dma = pltpu.SemaphoreType.DMA
    out = pl.pallas_call(
        functools.partial(kernel, ns),
        out_shape=jax.ShapeDtypeStruct((LOCAL * 8, 128), F32),
        in_specs=[hbm, vmem, vmem, pl.BlockSpec(memory_space=pltpu.SMEM), hbm, hbm, vmem],
        out_specs=hbm,
        scratch_shapes=[
            pltpu.VMEM((LOCAL * 8, 128), F32),
            pltpu.VMEM((LOCAL * 8, 128), F32),
            pltpu.VMEM((2, BINS, BINS), BF16),
            pltpu.VMEM((12, BINS, 256), BF16),
            pltpu.VMEM((12, 1536, 256), BF16),
            pltpu.VMEM((2048, 512), BF16),
            pltpu.VMEM((NSPEC, 192, 176), BF16),
            pltpu.VMEM((12, 12, 24, 128), F32),
            pltpu.VMEM((12, 12, 24, 128), F32),
            pltpu.VMEM((12, 128, 128), F32),
            pltpu.VMEM((12, 128, 256), F32),
            pltpu.VMEM((128, 1536), BF16),
            pltpu.VMEM((128, 1536), BF16),
            pltpu.VMEM((12, 128, 128), F32),
            pltpu.VMEM((12, 8, 128), F32),
            pltpu.VMEM((16, 32, 128), F32),
            pltpu.VMEM((3, 16, 128), F32),
            pltpu.VMEM((8, ROWS, 128), F32),
            pltpu.VMEM((8, ROWS, 128), F32),
            pltpu.VMEM((8, ROWS, 128), F32),
            pltpu.VMEM((12, 4, 16, 128), F32),
            pltpu.VMEM((12, 4, 8, 128), F32),
            pltpu.VMEM((12, 8, 128), F32),
            pltpu.VMEM((PHASES, 12, 4, 16, 128), F32),
            pltpu.VMEM((PHASES, 12, 4, 8, 128), F32),
            pltpu.VMEM((PHASES, 12, 8, 128), F32),
            pltpu.VMEM((128, 128), F32),
            pltpu.VMEM((152, 128), F32),
            pltpu.VMEM((128, 128), F32),
            pltpu.VMEM((8, 128), F32),
            pltpu.VMEM((2, 8, 128), F32),
            dma((2,)), dma((8, 4)), dma((8, 4)), dma((8, 4)), dma((8, 4)), dma, dma, dma((4, 5)),
            dma((PHASES, 4, 3)), dma((PHASES, 4, 3)), dma((2,)), dma((2,)),
        ],
        compiler_params=pltpu.CompilerParams(
            collective_id=0, has_side_effects=True, vmem_limit_bytes=56 * 2**20),
        cost_estimate=pl.CostEstimate(flops=12 * 10**9, bytes_accessed=9 * 10**6, transcendentals=0),
        name="wave_steps",
    )(spectrum.reshape(LOCAL * 8, 128), ocean_mask, depth_class, freq_speed, coupling, source, gain_table)
    return out.reshape(LOCAL, 8, 128)


def solution(mesh):
    placed = (P("spec", "space", None), P("space", None), P("space", None), P(), P(), P(), P())
    return jax.shard_map(
        functools.partial(shards, mesh.shape["space"]), mesh=mesh, in_specs=placed,
        out_specs=P("spec", "space", None), check_vma=False)
```

```python
import functools
import math

import jax
import jax.numpy as jnp
from jax import lax
from jax.experimental import pallas as pl
from jax.experimental.pallas import tpu as pltpu
from jax.sharding import PartitionSpec as P

MESH = pl.DeviceIdType.MESH
F32, BF16, I32 = jnp.float32, jnp.bfloat16, jnp.int32
BINS, NDIR, NFREQ, CLASSES = 1296, 36, 36, 8
ITERS = 4
NSPEC, LOCAL = 8, 162
SLOT = 48
FULL = (5, 5, 4, 4)
BASE = (0, 48, 96, 136)
KEPT = (48, 48, 40, 40)
LIVE = (45, 45, 36, 36)
ROWS = 176
QUADS = (0, 2, 1, 3)
LOWX, LOWY = (True, False, False, True), (True, False, True, False)
PAIRS = ((0, 0), (1, 0), (1, 1), (2, 1), (3, 1), (3, 2), (4, 2), (5, 2))
PHASES = ITERS + 1


def off_j(q):
    return 4 if LOWY[q] else 0


def off_i(q):
    return 8 if LOWX[q] else 0


def block_of(r, half):
    low = lax.rem(r // 4 + half, 2)
    x = lax.rem(r, 4)
    return jnp.where(low == 0, x, 7 - x)


def owner_of(c, half):
    x = jnp.where(c < 4, c, 7 - c)
    return lax.rem(c // 4 + half, 2) * 4 + x


def swap_blocks(parts):
    lane = lax.broadcasted_iota(I32, parts[0].shape, 1)
    for h in (4, 2, 1):
        keep = (lane & (16 * h)) == 0
        new = list(parts)
        for j in range(8):
            if j & h == 0:
                a, b = parts[j], parts[j + h]
                new[j] = jnp.where(keep, a, pltpu.roll(b, 16 * h, 1))
                new[j + h] = jnp.where(keep, pltpu.roll(a, 128 - 16 * h, 1), b)
        parts = new
    return parts


def local_bin(rel, idx):
    many = rel < 2
    whole = jnp.where(many, 40, 32)
    runs = jnp.where(many, 5, 4)
    first = 36 * (idx >> 3) + (idx & 7)
    last = 36 * (idx - whole) + 8
    return jnp.where(idx < whole, first + 9 * rel, jnp.where(idx < whole + runs, last + 9 * rel, -10000))


def places(q, g, shape):
    slot = 128 * g + lax.broadcasted_iota(I32, shape, len(shape) - 1)
    r = jnp.zeros_like(slot)
    for k in range(1, 8):
        r = r + (slot >= SLOT * k).astype(I32)
    return r, q ^ (2 * (r & 1)), slot - SLOT * r


def relative(q, r):
    return QUADS[q] ^ (2 * (r & 1))


def kernel(ns, spectrum_ref, mask_ref, class_ref, speed_ref, coupling_ref, source_ref, gain_ref, result_ref,
           x_ref, out_ref, natural, turned, weights, pick, lift, e0, e1, slope, part, xb, yb, gains, gain_rows, mask, coef,
           send_a, land_a, land_b, ys, xs, cs, yl, xl, cl, tile, strip, kind, mask_own, mask_land,
           w_sem, a_send, a_recv, b_send, b_recv, own_sem, x_sem, o_sem, h_send, h_recv, m_send, m_recv):
    r = lax.axis_index("spec")
    s = lax.axis_index("space")
    half = s // (ns // 2)
    c = block_of(r, half)

    def at(dc, ds):
        cc, ss = jnp.clip(c + dc, 0, NSPEC - 1), jnp.clip(s + ds, 0, ns - 1)
        return (ss, owner_of(cc, ss // (ns // 2)))

    def there(dc, ds):
        ok = None
        for cond in ([c + dc >= 0, c + dc < NSPEC] if dc else []) + ([s + ds >= 0, s + ds < ns] if ds else []):
            ok = cond if ok is None else jnp.logical_and(ok, cond)
        return ok

    take_x = pltpu.make_async_copy(spectrum_ref, x_ref, x_sem)
    take_x.start()
    loads = [pltpu.make_async_copy(ref, natural.at[m], w_sem.at[m]) for m, ref in enumerate((coupling_ref, source_ref))]
    for slot in range(NSPEC):
        for rel in range(4):
            end = BASE[rel] + KEPT[rel]
            land_a[slot, end - 8:end, :] = jnp.zeros((8, 128), F32)
    barrier = pltpu.get_barrier_semaphore()
    around = [(dc, ds) for ds in (-1, 1) for dc in (-1, 0, 1)]
    for k in range(1, NSPEC):
        pl.semaphore_signal(barrier, inc=1, device_id=(s, lax.rem(r + k, NSPEC)), device_id_type=MESH)
    for dc, ds in around:
        @pl.when(there(dc, ds))
        def _():
            pl.semaphore_signal(barrier, inc=1, device_id=at(dc, ds), device_id_type=MESH)

    for copy in loads:
        copy.start()
    mask_own[...] = mask_ref[...].astype(F32)

    def clear(qg, _):
        e0[qg] = jnp.zeros((12, 24, 128), F32)
        e1[qg] = jnp.zeros((12, 24, 128), F32)
        return 0
    lax.fori_loop(0, 12, clear, 0)
    take_x.wait()

    for rel in range(4):
        for f in range(FULL[rel]):
            parts = [x_ref[pl.ds((36 * f + 9 * rel) * 8 + j, 8, stride=8), :] for j in range(8)]
            for cc, block in enumerate(swap_blocks(parts)):
                send_a[cc, BASE[rel] + 8 * f:BASE[rel] + 8 * f + 8, :] = block
        n = FULL[rel]
        parts = [x_ref[pl.ds((9 * rel + 8) * 8 + j, n, stride=288), :] for j in range(8)]
        for cc, block in enumerate(swap_blocks(parts)):
            send_a[cc, BASE[rel] + 8 * n:BASE[rel] + 8 * n + 8, :] = jnp.zeros((8, 128), F32)
            send_a[cc, BASE[rel] + 8 * n:BASE[rel] + 9 * n, :] = block

    beside = (c > 0).astype(I32) + (c < NSPEC - 1).astype(I32)
    beyond = (s > 0).astype(I32) + (s < ns - 1).astype(I32)
    pl.semaphore_wait(barrier, NSPEC - 1 + beyond * (1 + beside))

    def a_copy(k, rel, incoming=False):
        peer = lax.rem(r + k, NSPEC)
        slot = peer if incoming else r
        rows = pl.ds(BASE[rel], LIVE[rel])
        return pltpu.make_async_remote_copy(
            src_ref=send_a.at[block_of(peer, half), rows], dst_ref=land_a.at[slot, rows],
            send_sem=a_send.at[k, rel], recv_sem=a_recv.at[slot, rel], device_id=(s, peer), device_id_type=MESH)

    for rel in range(4):
        for k in range(1, NSPEC):
            a_copy(k, rel).start()
    own_a = pltpu.make_async_copy(send_a.at[c], land_a.at[r], own_sem)
    own_a.start()

    def mask_copy(ds, incoming=False):
        k = (1 if ds < 0 else 0) if not incoming else (0 if ds < 0 else 1)
        return pltpu.make_async_remote_copy(
            src_ref=mask_own, dst_ref=mask_land.at[k], send_sem=m_send.at[k], recv_sem=m_recv.at[k],
            device_id=at(0, ds), device_id_type=MESH)

    for ds in (-1, 1):
        @pl.when(there(0, ds))
        def _():
            mask_copy(ds).start()

    row = lax.broadcasted_iota(I32, (16, 128), 0)
    quad = (row >= 3).astype(I32) + (row >= 6).astype(I32) + (row >= 9).astype(I32)
    group = row - 3 * quad
    quad = jnp.where(quad == 1, 2, jnp.where(quad == 2, 1, quad))
    home, rel, idx = places(quad, group, (16, 128))
    here = local_bin(rel, idx)
    many = rel < 2
    whole = jnp.where(many, 40, 32)
    run = jnp.where(idx < whole, idx >> 3, idx - whole)
    step = jnp.where(idx < whole, idx & 7, 8)
    freq = ((9 * home) >> 1) + run + jnp.where(many, 0, home & 1)
    group_speed = jnp.zeros((16, 128), F32)
    for k in range(NFREQ):
        group_speed = jnp.where(freq == k, speed_ref[k], group_speed)
    group_speed = jnp.where(here >= 0, group_speed, 0.0)
    cosine, sine = jnp.zeros((16, 128), F32), jnp.zeros((16, 128), F32)
    for k in range(9):
        cosine = jnp.where(step == k, math.cos(2.0 * math.pi * (k + 0.5) / NDIR), cosine)
        sine = jnp.where(step == k, math.sin(2.0 * math.pi * (k + 0.5) / NDIR), sine)
    even = (quad & 1) == 0
    ax = group_speed * jnp.where(even, cosine, sine)
    ay = group_speed * jnp.where(even, sine, cosine)
    coef[0] = 1.0 - ax - ay
    coef[1] = ax
    coef[2] = ay

    for k, (t, g) in enumerate(PAIRS):
        rows = 16 if t == 5 else 256
        for q in range(4):
            home, rel, idx = places(jnp.full((1, 128), QUADS[q], I32), g, (1, 128))
            want = LOCAL * home + local_bin(rel, idx) - 256 * t
            hit = lax.broadcasted_iota(I32, (rows, 128), 0) == want
            pick[256 * k:256 * k + rows, 128 * q:128 * q + 128] = jnp.where(hit, 1.0, 0.0).astype(BF16)

    def to_quadrants(lhs, g):
        first, start, depth = ((0, 0, 512), (2, 256, 768), (5, 768, 528))[g]
        return jnp.dot(lhs(start, depth), pick[256 * first:256 * first + depth, :], preferred_element_type=F32)

    for rr in range(NSPEC):
        for q in range(4):
            spot = lax.broadcasted_iota(I32, (SLOT, 176), 0)
            want = local_bin(jnp.full((SLOT, 176), relative(q, rr), I32), spot) + 2 * rr
            hit = lax.broadcasted_iota(I32, (SLOT, 176), 1) == want
            lift[rr, SLOT * q:SLOT * q + SLOT, :] = jnp.where(hit, 1.0, 0.0).astype(BF16)

    table = gain_ref[...]
    high = table.astype(BF16).astype(F32)
    mid = (table - high).astype(BF16).astype(F32)
    low = table - high - mid
    thirds = jnp.concatenate([high, mid, low, jnp.zeros_like(low)], axis=0).astype(BF16)
    for g in range(3):
        total = to_quadrants(lambda at_, n: thirds[:, at_:at_ + n], g)
        for q in range(4):
            third = total[:, 128 * q:128 * q + 128]
            gain_rows[3 * q + g] = third[0:8] + third[8:16] + third[16:24]

    for copy in loads:
        copy.wait()
    for m in range(2):
        def columns(k, _, m=m):
            rows = pl.ds(pl.multiple_of(432 * k, 16), 432)
            for g in range(3):
                total = to_quadrants(lambda at_, n: natural[m, rows, at_:at_ + n], g).astype(BF16)
                for q in range(4):
                    turned[3 * q + g, rows, 128 * m:128 * m + 128] = total[:, 128 * q:128 * q + 128]
            return 0
        lax.fori_loop(0, 3, columns, 0)

    for k, ds in ((0, -1), (1, 1)):
        @pl.when(there(0, ds))
        def _():
            mask_copy(ds, incoming=True).wait_recv()
            mask_copy(ds).wait_send()
            tile[16 * k:16 * k + 8, :] = mask_land[k]

        @pl.when(jnp.logical_not(there(0, ds)))
        def _():
            tile[16 * k:16 * k + 8, :] = jnp.zeros((8, 128), F32)
    tile[8:16, :] = mask_own[...]
    tile[24:32, :] = class_ref[...].astype(F32)
    tile[32:128, :] = jnp.zeros((96, 128), F32)
    strip[0:8, :] = jnp.zeros((8, 128), F32)
    strip[136:152, :] = jnp.zeros((16, 128), F32)
    strip[8:136, :] = tile[...].T
    near = strip[pl.ds(pl.multiple_of(16 * c, 16), 32), :]
    for j in range(16):
        mask[j] = jnp.broadcast_to(near[:, j + 4:j + 5], (32, 128))
    for j in range(8):
        kind[16 * j:16 * j + 16, :] = jnp.broadcast_to(near[8:24, 24 + j:25 + j], (16, 128))

    def fill(qg, _):
        which = kind[...]
        value = jnp.zeros((128, 128), F32)
        for k in range(CLASSES):
            value = jnp.where(which == float(k), gain_rows[qg, k:k + 1, :], value)
        gains[qg] = value
        return 0
    lax.fori_loop(0, 12, fill, 0)

    def heading(q):
        return (1 if LOWX[q] else -1), (1 if LOWY[q] else -1)

    def edge(q, kind):
        dx, dy = heading(q)
        return ((0, dy), (dx, 0), (dx, dy))[kind]

    def edge_copy(p, q, kind):
        dc, ds = edge(q, kind)
        groups = pl.ds(3 * q, 3)
        src, dst = ((ys, yl), (xs, xl), (cs, cl))[kind]
        return pltpu.make_async_remote_copy(
            src_ref=src.at[groups], dst_ref=dst.at[p, groups], send_sem=h_send.at[p, q, kind],
            recv_sem=h_recv.at[p, q, kind], device_id=at(dc, ds), device_id_type=MESH)

    def corner(q, landed):
        for d, (n, at_) in enumerate(((3, 0), (2, 3), (1, 5))):
            j = (3 - d if landed else 11 - d) if LOWY[q] else (8 + d if landed else d)
            i = ((8 if landed else 24) - n) if LOWX[q] else (16 if landed else 0)
            yield n, at_, j, i

    def send_edges(p, q):
        i = 20 if LOWX[q] else 0
        jy = 8 if LOWY[q] else 0
        groups = range(3 * q, 3 * q + 3)

        def start(kind):
            @pl.when(there(*edge(q, kind)))
            def _():
                edge_copy(p, q, kind).start()

        for qg in groups:
            for n, at_, j, ii in corner(q, False):
                cs[qg, at_:at_ + n, :] = e0[qg, j, ii:ii + n, :]
        start(2)
        for qg in groups:
            for j in range(8):
                xs[qg, j // 2, 4 * (j % 2):4 * (j % 2) + 4, :] = e0[qg, off_j(q) + j, i:i + 4, :]
        start(1)
        for qg in groups:
            ys[qg] = e0[qg, jy:jy + 4, off_i(q):off_i(q) + 16, :]
        start(0)

    def take_edges(p, q):
        i = 4 if LOWX[q] else 16
        jh = 0 if LOWY[q] else 8
        groups = range(3 * q, 3 * q + 3)
        for kind in range(3):
            dc, ds = edge(q, kind)

            @pl.when(there(-dc, -ds))
            def _():
                edge_copy(p, q, kind).wait_recv()
                for qg in groups:
                    if kind == 0:
                        e0[qg, jh:jh + 4, off_i(q):off_i(q) + 16, :] = yl[p, qg]
                    elif kind == 1:
                        for j in range(8):
                            e0[qg, off_j(q) + j, i:i + 4, :] = xl[p, qg, j // 2, 4 * (j % 2):4 * (j % 2) + 4, :]
                    else:
                        for n, at_, j, ii in corner(q, True):
                            e0[qg, j, ii:ii + n, :] = cl[p, qg, at_:at_ + n, :]

    def settle_edges(p):
        for q in range(4):
            for kind in range(3):
                @pl.when(there(*edge(q, kind)))
                def _():
                    edge_copy(p, q, kind).wait_send()

    def substep(q, t):
        src, dst = (e0, e1) if t % 2 == 0 else (e1, e0)
        if LOWY[q]:
            j0, n, jm = t + 1, 11 - t, 0
        else:
            j0, n, jm = 0, 11 - t, 4
        if LOWX[q]:
            di, im, starts = -1, 0, (8, 16) + (() if t == 3 else (1,))
        else:
            di, im, starts = 1, 8, (0, 8) + (() if t == 3 else (15,))

        groups = slice(3 * q, 3 * q + 3)
        c0, cx, cy = (coef[k, groups, :].reshape(3, 1, 1, 128) for k in range(3))
        for i in starts:
            for first in range(j0, j0 + n, 4):
                m = min(4, j0 + n - first)
                if LOWY[q]:
                    both = src[groups, first - 1:first + m, i:i + 8, :]
                    mid, across = both[:, 1:], both[:, :-1]
                else:
                    both = src[groups, first:first + m + 1, i:i + 8, :]
                    mid, across = both[:, :-1], both[:, 1:]
                along = src[groups, first:first + m, i + di:i + di + 8, :]
                sea = mask[first + jm:first + jm + m, i + im:i + im + 8, :][None]
                dst[groups, first:first + m, i:i + 8, :] = (c0 * mid + cx * along + cy * across) * sea

    def interior(q):
        return slice(off_j(q), off_j(q) + 8), slice(off_i(q), off_i(q) + 16)

    def narrow(q):
        js, is_ = interior(q)
        for g in range(3):
            qg = 3 * q + g
            xb[:, 128 * qg:128 * qg + 128] = e0[qg, js, is_, :].reshape(128, 128).astype(BF16)

    def first_half(qg):
        part[qg] = jnp.dot(xb[:, :768], weights[qg, :768, :], preferred_element_type=F32)

    def second_half(qg):
        got = part[qg] + jnp.dot(xb[:, 768:], weights[qg, 768:, :], preferred_element_type=F32)
        change = gains[qg] * got[:, :128] + got[:, 128:]
        slope[qg] = change
        js, is_ = interior(qg // 3)
        state = e0[qg, js, is_, :].reshape(128, 128)
        yb[:, 128 * qg:128 * qg + 128] = (state + change).astype(BF16)

    def finish(q):
        js, is_ = interior(q)

        for qg in range(3 * q, 3 * q + 3):
            got = jnp.dot(yb[...], weights[qg], preferred_element_type=F32)
            change = gains[qg] * got[:, :128] + got[:, 128:]
            state = e0[qg, js, is_, :].reshape(128, 128)
            e0[qg, js, is_, :] = (state + 0.5 * (slope[qg] + change)).reshape(8, 16, 128)

    own_a.wait()
    for rel in range(4):
        for k in range(1, NSPEC):
            a_copy(k, rel, incoming=True).wait_recv()
    for q in range(4):
        for g in range(3):
            pieces = []
            for rr in range(NSPEC):
                a, b = max(SLOT * rr, 128 * g) - SLOT * rr, min(SLOT * rr + SLOT, 128 * g + 128) - SLOT * rr
                if a >= b:
                    continue
                rel = relative(q, rr)
                cut = min(b, KEPT[rel])
                if a < cut:
                    pieces.append(land_a[rr, BASE[rel] + a:BASE[rel] + cut, :])
                if cut < b:
                    pieces.append(jnp.zeros((b - max(a, cut), 128), F32))
            e0[3 * q + g, off_j(q):off_j(q) + 8, off_i(q):off_i(q) + 16, :] = (
                jnp.concatenate(pieces, axis=0).T.reshape(8, 16, 128))
        send_edges(0, q)

    def lines(qg, _):
        for rr in range(NSPEC):
            got = jnp.dot(lift[rr], turned[qg, 160 * rr:160 * rr + 176, :], preferred_element_type=F32).astype(BF16)
            for q in range(4):
                weights[qg, 384 * q + SLOT * rr:384 * q + SLOT * rr + SLOT, :] = got[SLOT * q:SLOT * q + SLOT]
        return 0
    lax.fori_loop(0, 12, lines, 0)

    def phase(p, _):
        for q in range(4):
            take_edges(p, q)

            @pl.when(p > 0)
            def _():
                substep(q, 0)
                substep(q, 1)
            substep(q, 2)
            substep(q, 3)
            narrow(q)
            if q == 1:
                for qg in range(12):
                    first_half(qg)
        for qg in range(12):
            second_half(qg)
        settle_edges(p)
        for q in range(4):
            finish(q)
            send_edges(p + 1, q)
        return 0

    lax.fori_loop(0, ITERS, phase, 0)

    for rel in range(4):
        for k in range(1, NSPEC):
            a_copy(k, rel).wait_send()

    def b_copy(k, q, odd, incoming=False):
        peer = lax.rem(r + k, NSPEC)
        slot = block_of(peer, half) if incoming else c
        rel = relative(q, odd)
        rows = pl.ds(BASE[rel], LIVE[rel])
        return pltpu.make_async_remote_copy(
            src_ref=send_a.at[peer, rows], dst_ref=land_b.at[slot, rows],
            send_sem=b_send.at[k, q], recv_sem=b_recv.at[slot, rel], device_id=(s, peer), device_id_type=MESH)

    for q in range(4):
        take_edges(ITERS, q)
        substep(q, 2)
        substep(q, 3)
        js, is_ = interior(q)
        for g in range(3):
            block = e0[3 * q + g, js, is_, :].reshape(128, 128).T
            for rr in range(NSPEC):
                a, b = max(SLOT * rr, 128 * g), min(SLOT * rr + SLOT, 128 * g + 128)
                rel = relative(q, rr)
                b = min(b, SLOT * rr + KEPT[rel])
                if a < b:
                    send_a[rr, BASE[rel] + a - SLOT * rr:BASE[rel] + b - SLOT * rr, :] = block[a - 128 * g:b - 128 * g]
        for k in range(1, NSPEC):
            for odd in range(2):
                @pl.when(lax.rem(r + k, 2) == odd)
                def _():
                    b_copy(k, q, odd).start()
    settle_edges(ITERS)
    own_b = pltpu.make_async_copy(send_a.at[r], land_b.at[c], own_sem)
    own_b.start()

    def put(rel):
        n = FULL[rel]
        for f in range(n):
            rows = slice(BASE[rel] + 8 * f, BASE[rel] + 8 * f + 8)
            parts = swap_blocks([land_b[cc, rows, :] for cc in range(8)])
            for j in range(8):
                out_ref[pl.ds((36 * f + 9 * rel) * 8 + j, 8, stride=8), :] = parts[j]
        parts = swap_blocks([land_b[cc, BASE[rel] + 8 * n:BASE[rel] + 9 * n, :] for cc in range(8)])
        for j in range(8):
            out_ref[pl.ds((9 * rel + 8) * 8 + j, n, stride=288), :] = parts[j]
        for f in range(n):
            out_copy(rel, f).start()

    def out_copy(rel, f):
        rows = pl.ds((36 * f + 9 * rel) * 8, 72)
        return pltpu.make_async_copy(out_ref.at[rows], result_ref.at[rows], o_sem.at[rel, f])

    own_b.wait()
    for odd in range(2):
        @pl.when(lax.rem(r, 2) == odd)
        def _():
            for q in range(4):
                for k in range(1, NSPEC):
                    b_copy(k, q, odd, incoming=True).wait_recv()
                put(relative(q, odd))
    for k in range(1, NSPEC):
        for q in range(4):
            for odd in range(2):
                @pl.when(lax.rem(r + k, 2) == odd)
                def _():
                    b_copy(k, q, odd).wait_send()
    for rel in range(4):
        for f in range(FULL[rel]):
            out_copy(rel, f).wait()


def shards(ns, spectrum, ocean_mask, depth_class, freq_speed, coupling, source, gain_table):
    vmem, hbm = pl.BlockSpec(memory_space=pltpu.VMEM), pl.BlockSpec(memory_space=pl.ANY)
    dma = pltpu.SemaphoreType.DMA
    out = pl.pallas_call(
        functools.partial(kernel, ns),
        out_shape=jax.ShapeDtypeStruct((LOCAL * 8, 128), F32),
        in_specs=[hbm, vmem, vmem, pl.BlockSpec(memory_space=pltpu.SMEM), hbm, hbm, vmem],
        out_specs=hbm,
        scratch_shapes=[
            pltpu.VMEM((LOCAL * 8, 128), F32),
            pltpu.VMEM((LOCAL * 8, 128), F32),
            pltpu.VMEM((2, BINS, BINS), BF16),
            pltpu.VMEM((12, BINS, 256), BF16),
            pltpu.VMEM((12, 1536, 256), BF16),
            pltpu.VMEM((2048, 512), BF16),
            pltpu.VMEM((NSPEC, 192, 176), BF16),
            pltpu.VMEM((12, 12, 24, 128), F32),
            pltpu.VMEM((12, 12, 24, 128), F32),
            pltpu.VMEM((12, 128, 128), F32),
            pltpu.VMEM((12, 128, 256), F32),
            pltpu.VMEM((128, 1536), BF16),
            pltpu.VMEM((128, 1536), BF16),
            pltpu.VMEM((12, 128, 128), F32),
            pltpu.VMEM((12, 8, 128), F32),
            pltpu.VMEM((16, 32, 128), F32),
            pltpu.VMEM((3, 16, 128), F32),
            pltpu.VMEM((8, ROWS, 128), F32),
            pltpu.VMEM((8, ROWS, 128), F32),
            pltpu.VMEM((8, ROWS, 128), F32),
            pltpu.VMEM((12, 4, 16, 128), F32),
            pltpu.VMEM((12, 4, 8, 128), F32),
            pltpu.VMEM((12, 8, 128), F32),
            pltpu.VMEM((PHASES, 12, 4, 16, 128), F32),
            pltpu.VMEM((PHASES, 12, 4, 8, 128), F32),
            pltpu.VMEM((PHASES, 12, 8, 128), F32),
            pltpu.VMEM((128, 128), F32),
            pltpu.VMEM((152, 128), F32),
            pltpu.VMEM((128, 128), F32),
            pltpu.VMEM((8, 128), F32),
            pltpu.VMEM((2, 8, 128), F32),
            dma((2,)), dma((8, 4)), dma((8, 4)), dma((8, 4)), dma((8, 4)), dma, dma, dma((4, 5)),
            dma((PHASES, 4, 3)), dma((PHASES, 4, 3)), dma((2,)), dma((2,)),
        ],
        compiler_params=pltpu.CompilerParams(
            collective_id=0, has_side_effects=True, vmem_limit_bytes=56 * 2**20),
        cost_estimate=pl.CostEstimate(flops=12 * 10**9, bytes_accessed=9 * 10**6, transcendentals=0),
        name="wave_steps",
    )(spectrum.reshape(LOCAL * 8, 128), ocean_mask, depth_class, freq_speed, coupling, source, gain_table)
    return out.reshape(LOCAL, 8, 128)


def solution(mesh):
    placed = (P("spec", "space", None), P("space", None), P("space", None), P(), P(), P(), P())
    return jax.shard_map(
        functools.partial(shards, mesh.shape["space"]), mesh=mesh, in_specs=placed,
        out_specs=P("spec", "space", None), check_vma=False)
```
